256 devices in a mesh: dp: 8 (over y, core), fsdp: 32 (over x, z).
Axes of the slice: x: 4, y: 4, z: 8, core: 2. Of those that a mesh axis runs over, the one named last changes fastest.
Arguments:
- activations: bfloat16 [81920, 8192], P(('dp', 'fsdp')), may hold values from -16 to 16
- cotangent: bfloat16 [81920, 512], P(('dp', 'fsdp')), may hold values from -6 to 6
- kv_weight: bfloat16 [8192, 512], P('fsdp'), may hold values from -0.25 to 0.25
- error_buffer: float32 [8, 8192, 512], P('dp', 'fsdp'), may hold values from -6 to 6
- q_start: float32 [64, 512], replicated, may hold values from -6 to 6
Outputs:
- input_grad: bfloat16 [81920, 8192], P(('dp', 'fsdp'))
- error_next: float32 [8, 8192, 512], P('dp', 'fsdp')
- compressed: float32 [8192, 512], P('fsdp')
- q_next: float32 [64, 512], replicated
The draws below stay inside these ranges and needn't reach their ends.
All inputs are finite; a program needn't handle non-finite values.
Results may differ from the reference program's by a relative error of at most 0.0004.
Values may be sent and summed in bfloat16 or wider, within the bound.
No kernel may reach another device: no remote copies, remote signals or barrier semaphores. Data moves between devices by JAX's collectives and lax.ppermute only.
A program may use at most 128 MiB of HBM per device.

```python
import math
import jax
import jax.numpy as jnp
from jax import lax

D = 8192
R = 64
KV = 512
GROUP_TOK = 10240
TOKENS = 81920
N_DP = 8


def draw_activations(key, part):
    key = jax.random.fold_in(key, 11)
    key_cols, key_vals = jax.random.split(key, 2)
    position = jnp.arange(D, dtype=jnp.float32) / D
    col_scale = 0.3 * jnp.exp(position * math.log(3.0) + jax.random.uniform(key_cols, (D,), jnp.float32, 0.0, math.log(3.3)))
    base_vals = jnp.clip(jax.random.normal(key_vals, (TOKENS, D), jnp.float32), -5.0, 5.0)
    return (base_vals * col_scale[None, :]).astype(jnp.bfloat16)


def level_of(key, dims, shards, smallest, largest):
    def one(dim, blocks):
        draws = jax.random.uniform(jax.random.fold_in(jax.random.fold_in(key, 6), dim), (blocks,), jnp.float32, smallest / len(shards), largest / len(shards))
        return jnp.repeat(jnp.exp(draws), dims[dim] // blocks).reshape((-1,) + (1,) * (len(dims) - dim - 1))

    factor_of = one(*shards[0])
    for cut in shards[1:]:
        factor_of = factor_of * one(*cut)
    return factor_of


def scatter_about(own_key, dims, scale, bound, cuts=(), kind=jnp.bfloat16):
    result = jax.random.normal(own_key, dims, jnp.float32) * scale
    if len(cuts) > 0:
        result = level_of(own_key, dims, cuts, -0.22, 0.18) * result
    return jnp.clip(result, min=-bound, max=bound).astype(kind)


def setup_inputs(seed: int = 0) -> dict:
    arg_keys = jax.random.split(jax.random.key(seed), 6)
    return {
        "activations": draw_activations(jax.random.fold_in(arg_keys[5], 71), 0),
        "cotangent": scatter_about(arg_keys[1], (TOKENS, KV), 1.0, 6.0, ((0, 256),)),
        "kv_weight": scatter_about(arg_keys[2], (D, KV), KV ** -0.5, 0.25, ((0, 32),)),
        "error_buffer": scatter_about(arg_keys[3], (N_DP, D, KV), 1.0, 6.0, ((0, 8), (1, 32)), jnp.float32),
        "q_start": scatter_about(arg_keys[4], (R, KV), 1.0, 6.0, (), jnp.float32),
    }


loss_scale = 256.0

def reference(activations, cotangent, kv_weight, error_buffer, q_start):
    highest = lax.Precision.HIGHEST
    input_grad = jnp.dot(cotangent.astype(jnp.float32), kv_weight.T.astype(jnp.float32), preferred_element_type=jnp.float32).astype(jnp.bfloat16)
    act_groups = activations.reshape(N_DP, GROUP_TOK, D)
    cot_groups = cotangent.reshape(N_DP, GROUP_TOK, KV)
    merged_all = []
    p_total = jnp.zeros((R, D), jnp.float32)
    for replica in range(N_DP):
        gradient = jnp.dot(act_groups[replica].T.astype(jnp.float32), cot_groups[replica].astype(jnp.float32), preferred_element_type=jnp.float32) / loss_scale
        merged = gradient + error_buffer[replica]
        merged_all.append(merged)
        p_total = p_total + jnp.dot(q_start, merged.T, precision=highest)
    gram_matrix = jnp.dot(p_total, p_total.T, precision=highest)
    factor_low = jnp.linalg.cholesky(gram_matrix)
    p_basis = lax.linalg.triangular_solve(factor_low, p_total, left_side=True, lower=True)
    q_next = jnp.zeros((R, KV), jnp.float32)
    for merged in merged_all:
        q_next = q_next + jnp.dot(p_basis, merged, precision=highest)
    q_next = q_next / N_DP
    compressed = jnp.dot(p_basis.T, q_next, precision=highest)
    error_next = jnp.stack([merged - compressed for merged in merged_all])
    return (input_grad, error_next, compressed, q_next)
```

```python
import jax
import jax.numpy as jnp
from jax import lax
from jax.experimental import pallas as pl
from jax.experimental.pallas import tpu as pltpu
from jax.sharding import Mesh, PartitionSpec as P

LOSS_SCALE = 256.0
HIGHEST = lax.Precision.HIGHEST
F32 = jnp.float32
BF16 = jnp.bfloat16
NY, NC, NX, NZ = 4, 2, 4, 8
NT = (((1,), (1,)), ((), ()))
TN = (((0,), (0,)), ((), ()))


def swap(value, axis, size, k):
    return lax.ppermute(value, axis, [(i, i ^ k) for i in range(size)])


def swaps(value, axis, size):
    return [value] + [swap(value, axis, size, k) for k in range(1, size)]


def tree(parts):
    while len(parts) > 1:
        parts = [parts[i] + parts[i + 1] for i in range(0, len(parts), 2)]
    return parts[0]


def project_kernel(place, cot, *rest):
    pieces, out, rows, arrived = rest[:NC * NX], rest[NC * NX], rest[NC * NX + 1], rest[NC * NX + 2]
    sub = pieces[0].shape[1]
    block = NC * sub

    def fetch(k, c):
        start = pl.multiple_of((place[1] ^ c) * sub, sub)
        return pltpu.make_async_copy(
            pieces[NC * k + c], rows.at[k, :, pl.ds(start, sub), :], arrived.at[NC * k + c]
        )

    @pl.when(pl.program_id(0) == 0)
    def _():
        for k in range(NX):
            for c in range(NC):
                fetch(k, c).start()

    for k in range(NX):
        @pl.when(pl.program_id(0) == k)
        def _():
            for c in range(NC):
                fetch(k, c).wait()
            for z in range(NZ):
                out[:, z * block:(z + 1) * block] = lax.dot_general(
                    cot[...], rows[k, z], NT, preferred_element_type=F32
                ).astype(BF16)


def project(place, cot, pieces):
    tokens, width = cot.shape
    sub = pieces[0].shape[1]
    columns = NZ * NC * sub
    return pl.pallas_call(
        project_kernel,
        out_shape=jax.ShapeDtypeStruct((tokens, NX * columns), BF16),
        grid_spec=pltpu.PrefetchScalarGridSpec(
            num_scalar_prefetch=1,
            grid=(NX,),
            in_specs=[pl.BlockSpec((tokens, width), lambda k, place: (0, 0))]
            + [pl.BlockSpec(memory_space=pl.ANY)] * (NC * NX),
            out_specs=pl.BlockSpec((tokens, columns), lambda k, place: (0, k ^ place[0])),
            scratch_shapes=[pltpu.VMEM((NX, NZ, NC * sub, width), BF16), pltpu.SemaphoreType.DMA((NC * NX,))],
        ),
        cost_estimate=pl.CostEstimate(
            flops=2 * tokens * width * NX * columns,
            bytes_accessed=2 * (tokens + width) * NX * columns,
            transcendentals=0,
        ),
        compiler_params=pltpu.CompilerParams(vmem_limit_bytes=40 * 1024 * 1024),
        name="project",
    )(place, cot, *pieces)


def right_kernel(place, _, gradient, error, p_total, merged_out, keep, give):
    half = keep.shape[0]
    merged = gradient[...] * (1.0 / LOSS_SCALE) + error[...]
    merged_out[...] = merged
    p = p_total[...]
    right = jnp.dot(p, merged, precision=HIGHEST, preferred_element_type=F32)
    gram = lax.dot_general(p, p, NT, precision=HIGHEST, preferred_element_type=F32) * (1.0 / (NY * NC))
    sums = jnp.concatenate([right, gram], axis=1)
    first = place[1] == 0
    keep[...] = jnp.where(first, sums[:half], sums[half:])
    give[...] = jnp.where(first, sums[half:], sums[:half])


def right_terms(place, after, gradient, error, p_total):
    rank, width = p_total.shape[0], gradient.shape[1]
    half = jax.ShapeDtypeStruct((rank // NC, width + rank), F32)
    return pl.pallas_call(
        right_kernel,
        out_shape=(jax.ShapeDtypeStruct(gradient.shape, F32), half, half),
        in_specs=[pl.BlockSpec(memory_space=pltpu.SMEM), pl.BlockSpec(memory_space=pltpu.HBM)]
        + [pl.BlockSpec(memory_space=pltpu.VMEM)] * 3,
        compiler_params=pltpu.CompilerParams(vmem_limit_bytes=32 * 1024 * 1024),
        name="right_terms",
    )(place, after, gradient, error, p_total)


def finish_kernel(place, mine, other, p_total, merged, error_out, compressed_out, q_out):
    rank, width = p_total.shape[0], merged.shape[1]
    first = place[1] == 0
    sums = jnp.concatenate([jnp.where(first, mine[...], other[...]), jnp.where(first, other[...], mine[...])], axis=0)
    gram = sums[:, width:]
    row = lax.broadcasted_iota(jnp.int32, (rank, 2 * rank), 0)
    col = lax.broadcasted_iota(jnp.int32, (rank, 2 * rank), 1)
    work = jnp.concatenate([gram, jnp.zeros_like(gram)], axis=1)
    work = jnp.where(col == row + rank, 1.0, work)
    scale = jnp.zeros((rank, 1), F32)
    row1 = lax.broadcasted_iota(jnp.int32, (rank, 1), 0)
    for k in range(rank):
        pivot = work[k:k + 1, k:k + 1]
        ratio = jnp.where(row1 > k, work[:, k:k + 1] * (1.0 / pivot), 0.0)
        scale = jnp.where(row1 == k, lax.rsqrt(pivot), scale)
        work = work - ratio * work[k:k + 1, :]
    inverse = work[:, rank:] * scale
    q_next = jnp.dot(inverse, sums[:, :width], precision=HIGHEST, preferred_element_type=F32) * (1.0 / (NY * NC))
    p_basis = jnp.dot(inverse, p_total[...], precision=HIGHEST, preferred_element_type=F32)
    compressed = lax.dot_general(p_basis, q_next, TN, precision=HIGHEST, preferred_element_type=F32)
    q_out[...] = q_next
    compressed_out[...] = compressed
    error_out[...] = merged[...] - compressed


def finish(place, mine, other, p_total, merged):
    rank = p_total.shape[0]
    return pl.pallas_call(
        finish_kernel,
        out_shape=(
            jax.ShapeDtypeStruct(merged.shape, F32),
            jax.ShapeDtypeStruct(merged.shape, F32),
            jax.ShapeDtypeStruct((rank, merged.shape[1]), F32),
        ),
        in_specs=[pl.BlockSpec(memory_space=pltpu.SMEM)] + [pl.BlockSpec(memory_space=pltpu.VMEM)] * 4,
        compiler_params=pltpu.CompilerParams(vmem_limit_bytes=32 * 1024 * 1024),
        name="finish",
    )(place, mine, other, p_total, merged)


def thirds(value):
    parts = []
    for _ in range(3):
        part = lax.reduce_precision(value, 8, 7)
        parts.append(part.astype(BF16))
        value = value - part
    return jnp.concatenate(parts, axis=0)


def local(activations, cotangent, kv_weight, error_buffer, q_start):
    y, c, x, z = (lax.axis_index(a) for a in "ycxz")
    place = jnp.stack([x, c]).astype(jnp.int32)
    rank = q_start.shape[0]
    tokens = cotangent.shape[0]
    error = error_buffer[0]

    with jax.named_scope("exchange"):
        sub = kv_weight.shape[0] // NC
        mine = lax.dynamic_slice_in_dim(kv_weight, c * sub, sub, axis=0)
        line = lax.all_gather(mine, "z", axis=0)
        cot_x = jnp.zeros((NX * tokens, cotangent.shape[1]), BF16)
        for k, piece in enumerate(swaps(cotangent, "x", NX)):
            cot_x = lax.dynamic_update_slice_in_dim(cot_x, piece, (x ^ k) * tokens, axis=0)
        act_x = lax.all_to_all(activations, "x", 1, 0, tiled=True)

    with jax.named_scope("gradient"):
        part = jnp.einsum("td,tk->dk", act_x, cot_x, preferred_element_type=F32)
        part, line, act_x, cot_x = lax.optimization_barrier((part, line, act_x, cot_x))
        gradient = lax.psum_scatter(part, "z", scatter_dimension=0, tiled=True)

    with jax.named_scope("weight"):
        pieces = []
        for piece in swaps(line, "x", NX):
            pieces += [piece, swap(piece, "c", NC, 1)]
        input_grad = project(place, cotangent, pieces)

    with jax.named_scope("left"):
        q_cot = jnp.einsum("rk,tk->rt", q_start, cot_x.astype(F32), precision=HIGHEST)
        p_part = jnp.dot(thirds(q_cot), act_x, preferred_element_type=F32)
        p_part = p_part[:rank] + p_part[rank:2 * rank] + p_part[2 * rank:]
        p_part = lax.all_to_all(p_part, "z", 1, 0, tiled=True).reshape(NZ, rank, -1)
        p_own = jnp.einsum("rk,dk->rd", q_start, error, precision=HIGHEST)
        p_total = tree([p_part[i] for i in range(NZ)]) * (1.0 / LOSS_SCALE) + p_own
        p_total = tree(swaps(p_total, "c", NC))
        p_total = tree(swaps(p_total, "y", NY))

    with jax.named_scope("sums"):
        merged, keep, give = right_terms(place, input_grad[:16, :128], gradient, error, p_total)
        keep = keep + swap(give, "c", NC, 1)
        keep = tree(swaps(keep, "y", NY))
        keep = tree(swaps(keep, "x", NX))
        keep = keep + swap(keep, "z", NZ, 1)
        keep = tree([keep] + [swap(keep, "z", NZ, k) for k in (2, 4, 6)])
        other = swap(keep, "c", NC, 1)

    with jax.named_scope("finish"):
        error_next, compressed, q_next = finish(place, keep, other, p_total, merged)
    return (input_grad, error_next[None], compressed, q_next)


def solution(mesh):
    fine = Mesh(mesh.devices.reshape(NY, NC, NX, NZ), ("y", "c", "x", "z"))
    dp, fsdp = ("y", "c"), ("x", "z")
    return jax.shard_map(
        local,
        mesh=fine,
        in_specs=(P(dp + fsdp, None), P(dp + fsdp, None), P(fsdp, None), P(dp, fsdp, None), P()),
        out_specs=(P(dp + fsdp, None), P(dp, fsdp, None), P(fsdp, None), P()),
        check_vma=False,
    )
```

```python
import jax
import jax.numpy as jnp
from jax import lax
from jax.experimental import pallas as pl
from jax.experimental.pallas import tpu as pltpu
from jax.sharding import Mesh, PartitionSpec as P

LOSS_SCALE = 256.0
HIGHEST = lax.Precision.HIGHEST
F32 = jnp.float32
BF16 = jnp.bfloat16
NY, NC, NX, NZ = 4, 2, 4, 8
NT = (((1,), (1,)), ((), ()))
TN = (((0,), (0,)), ((), ()))


def swap(value, axis, size, k):
    return lax.ppermute(value, axis, [(i, i ^ k) for i in range(size)])


def swaps(value, axis, size):
    return [value] + [swap(value, axis, size, k) for k in range(1, size)]


def tree(parts):
    while len(parts) > 1:
        parts = [parts[i] + parts[i + 1] for i in range(0, len(parts), 2)]
    return parts[0]


def thirds(value):
    parts = []
    for _ in range(3):
        part = value.astype(BF16)
        parts.append(part)
        value = value - part.astype(F32)
    return jnp.concatenate(parts, axis=0)


def join(value):
    rank = value.shape[0] // 3
    return value[:rank] + (value[rank:2 * rank] + value[2 * rank:])


def pack_kernel(act, cot, out, done):
    columns = act.shape[1] // NX
    copies = []
    for i in range(NX):
        copies.append((act.at[:, pl.ds(i * columns, columns)], out.at[i, :, pl.ds(0, columns)]))
        copies.append((cot, out.at[i, :, pl.ds(columns, cot.shape[1])]))
    copies = [pltpu.make_async_copy(src, dst, done.at[i]) for i, (src, dst) in enumerate(copies)]
    for copy in copies:
        copy.start()
    for copy in copies:
        copy.wait()


def pack(activations, cotangent):
    tokens, width = cotangent.shape
    columns = activations.shape[1] // NX
    return pl.pallas_call(
        pack_kernel,
        out_shape=jax.ShapeDtypeStruct((NX, tokens, columns + width), BF16),
        in_specs=[pl.BlockSpec(memory_space=pltpu.HBM)] * 2,
        out_specs=pl.BlockSpec(memory_space=pltpu.HBM),
        scratch_shapes=[pltpu.SemaphoreType.DMA((2 * NX,))],
        name="pack",
    )(activations, cotangent)


def gradient_kernel(q, cot, act, gradient, left, lhs):
    rank, width = q.shape

    @pl.when(pl.program_id(0) == 0)
    def _():
        lhs[:width, :] = cot[...].T
        q_cot = lax.dot_general(
            q[...], cot[...].astype(F32), NT, precision=HIGHEST, preferred_element_type=F32
        )
        lhs[width:, :] = thirds(q_cot)

    both = jnp.dot(lhs[...], act[...], preferred_element_type=F32)
    gradient[0] = both[:width]
    left[0] = join(both[width:])


def gradient_terms(q_start, gathered):
    rank, width = q_start.shape
    tokens = gathered.shape[0]
    columns = gathered.shape[1] - width
    block = columns // NZ
    return pl.pallas_call(
        gradient_kernel,
        out_shape=(
            jax.ShapeDtypeStruct((NZ, width, block), F32),
            jax.ShapeDtypeStruct((NZ, rank, block), F32),
        ),
        grid=(NZ,),
        in_specs=[
            pl.BlockSpec((rank, width), lambda z: (0, 0)),
            pl.BlockSpec((tokens, width), lambda z: (0, columns // width)),
            pl.BlockSpec((tokens, block), lambda z: (0, z)),
        ],
        out_specs=(
            pl.BlockSpec((1, width, block), lambda z: (z, 0, 0)),
            pl.BlockSpec((1, rank, block), lambda z: (z, 0, 0)),
        ),
        scratch_shapes=[pltpu.VMEM((width + 3 * rank, tokens), BF16)],
        cost_estimate=pl.CostEstimate(
            flops=2 * (width + 3 * rank) * tokens * columns,
            bytes_accessed=2 * gathered.size + 4 * (width + rank) * columns,
            transcendentals=0,
        ),
        compiler_params=pltpu.CompilerParams(vmem_limit_bytes=60 * 1024 * 1024),
        name="gradient_terms",
    )(q_start, gathered, gathered)


def project_kernel(place, cot, own, other, out, rows, arrived):
    sub = own.shape[2]
    block = NC * sub

    def fetch(k, c):
        start = pl.multiple_of((place[1] ^ c) * sub, sub)
        return pltpu.make_async_copy(
            (own, other)[c].at[:, k], rows.at[k, :, pl.ds(start, sub), :], arrived.at[NC * k + c]
        )

    @pl.when(pl.program_id(0) == 0)
    def _():
        for k in range(NX):
            for c in range(NC):
                fetch(k, c).start()

    for k in range(NX):
        @pl.when(pl.program_id(0) == k)
        def _():
            for c in range(NC):
                fetch(k, c).wait()
            for z in range(NZ):
                out[:, z * block:(z + 1) * block] = lax.dot_general(
                    cot[...], rows[k, z], NT, preferred_element_type=F32
                ).astype(BF16)


def project(place, cot, own, other):
    tokens, width = cot.shape
    sub = own.shape[2]
    columns = NZ * NC * sub
    return pl.pallas_call(
        project_kernel,
        out_shape=jax.ShapeDtypeStruct((tokens, NX * columns), BF16),
        grid_spec=pltpu.PrefetchScalarGridSpec(
            num_scalar_prefetch=1,
            grid=(NX,),
            in_specs=[pl.BlockSpec((tokens, width), lambda k, place: (0, 0))]
            + [pl.BlockSpec(memory_space=pltpu.HBM)] * 2,
            out_specs=pl.BlockSpec((tokens, columns), lambda k, place: (0, k ^ place[0])),
            scratch_shapes=[pltpu.VMEM((NX, NZ, NC * sub, width), BF16), pltpu.SemaphoreType.DMA((NC * NX,))],
        ),
        cost_estimate=pl.CostEstimate(
            flops=2 * tokens * width * NX * columns,
            bytes_accessed=2 * (tokens + width) * NX * columns,
            transcendentals=0,
        ),
        compiler_params=pltpu.CompilerParams(vmem_limit_bytes=62_000_000),
        name="project",
    )(place, cot, own, other)


def right_kernel(place, _, cot, p_line, act, p_total, error, keep, give, inner):
    step = pl.program_id(0)
    half = keep.shape[0]
    part = join(lax.dot_general(thirds(p_line[0]), act[...], NT, preferred_element_type=F32))

    @pl.when(step == 0)
    def _():
        inner[...] = part

    @pl.when(step > 0)
    def _():
        inner[...] = inner[...] + part

    @pl.when(step == NZ - 1)
    def _():
        p = p_total[...]
        right = join(jnp.dot(thirds(inner[...]), cot[...], preferred_element_type=F32)) * (1.0 / LOSS_SCALE)
        right = right + jnp.dot(p, error[...], precision=HIGHEST, preferred_element_type=F32)
        gram = lax.dot_general(p, p, NT, precision=HIGHEST, preferred_element_type=F32) * (1.0 / (NY * NC))
        sums = jnp.concatenate([right, gram], axis=1)
        first = place[1] == 0
        keep[...] = jnp.where(first, sums[:half], sums[half:])
        give[...] = jnp.where(first, sums[half:], sums[:half])


def right_terms(place, after, gathered, p_line, p_total, error):
    rank, block = p_total.shape
    width = error.shape[1]
    tokens = gathered.shape[0]
    columns = gathered.shape[1] - width
    half = jax.ShapeDtypeStruct((rank // NC, width + rank), F32)
    whole = pl.BlockSpec((rank // NC, width + rank), lambda z, place: (0, 0))
    return pl.pallas_call(
        right_kernel,
        out_shape=(half, half),
        grid_spec=pltpu.PrefetchScalarGridSpec(
            num_scalar_prefetch=1,
            grid=(NZ,),
            in_specs=[
                pl.BlockSpec(memory_space=pltpu.HBM),
                pl.BlockSpec((tokens, width), lambda z, place: (0, columns // width)),
                pl.BlockSpec((1, rank, block), lambda z, place: (z, 0, 0)),
                pl.BlockSpec((tokens, block), lambda z, place: (0, z)),
                pl.BlockSpec((rank, block), lambda z, place: (0, 0)),
                pl.BlockSpec((block, width), lambda z, place: (0, 0)),
            ],
            out_specs=(whole, whole),
            scratch_shapes=[pltpu.VMEM((rank, tokens), F32)],
        ),
        cost_estimate=pl.CostEstimate(
            flops=6 * rank * tokens * (columns + width),
            bytes_accessed=2 * gathered.size,
            transcendentals=0,
        ),
        compiler_params=pltpu.CompilerParams(vmem_limit_bytes=32 * 1024 * 1024),
        name="right_terms",
    )(place, after, gathered, p_line, gathered, p_total, error)


def eliminate(gram):
    rank = gram.shape[0]
    group = 4
    row = lax.broadcasted_iota(jnp.int32, (rank, 2 * rank), 0)
    col = lax.broadcasted_iota(jnp.int32, (rank, 2 * rank), 1)
    work = jnp.where(col == row + rank, 1.0, jnp.concatenate([gram, jnp.zeros_like(gram)], axis=1))
    scale = jnp.zeros_like(work)
    for base in range(0, rank, group):
        at = [base + j for j in range(group)]
        cols = [jnp.broadcast_to(work[:, k:k + 1], work.shape) for k in at]
        rows = [work[k:k + 1, :] for k in at]
        for j, k in enumerate(at):
            pivot = cols[j][k:k + 1, :]
            ratio = jnp.where(row > k, cols[j] * (1.0 / pivot), 0.0)
            scale = jnp.where(row == k, lax.rsqrt(pivot), scale)
            for i in range(j + 1, group):
                cols[i] = cols[i] - ratio * cols[i][k:k + 1, :]
                rows[i] = rows[i] - ratio[at[i]:at[i] + 1, :] * rows[j]
            work = work - ratio * rows[j]
    return (work * scale)[:, rank:]


def finish_kernel(place, mine, other, p_total, gradient, error, error_out, compressed_out, q_out, own, old, arrived):
    width = error.shape[1]
    first = place[1] == 0
    fetches = [
        pltpu.make_async_copy(gradient.at[0], own, arrived.at[0]),
        pltpu.make_async_copy(error, old, arrived.at[1]),
    ]
    for fetch in fetches:
        fetch.start()
    sums = jnp.concatenate([jnp.where(first, mine[...], other[...]), jnp.where(first, other[...], mine[...])], axis=0)
    inverse = eliminate(sums[:, width:])
    q_next = jnp.dot(inverse, sums[:, :width], precision=HIGHEST, preferred_element_type=F32) * (1.0 / (NY * NC))
    p_basis = jnp.dot(inverse, p_total[...], precision=HIGHEST, preferred_element_type=F32)
    compressed = lax.dot_general(p_basis, q_next, TN, precision=HIGHEST, preferred_element_type=F32)
    q_out[...] = q_next
    compressed_out[...] = compressed
    for fetch in fetches:
        fetch.wait()
    error_out[...] = (own[...].T * (1.0 / LOSS_SCALE) + old[...]) - compressed


def finish(place, mine, other, p_total, gradient, error):
    rank = p_total.shape[0]
    return pl.pallas_call(
        finish_kernel,
        out_shape=(
            jax.ShapeDtypeStruct(error.shape, F32),
            jax.ShapeDtypeStruct(error.shape, F32),
            jax.ShapeDtypeStruct((rank, error.shape[1]), F32),
        ),
        in_specs=[pl.BlockSpec(memory_space=pltpu.SMEM)]
        + [pl.BlockSpec(memory_space=pltpu.VMEM)] * 3
        + [pl.BlockSpec(memory_space=pltpu.HBM)] * 2,
        scratch_shapes=[
            pltpu.VMEM(gradient.shape[1:], F32),
            pltpu.VMEM(error.shape, F32),
            pltpu.SemaphoreType.DMA((2,)),
        ],
        compiler_params=pltpu.CompilerParams(vmem_limit_bytes=62_800_000),
        name="finish",
    )(place, mine, other, p_total, gradient, error)


def local(activations, cotangent, kv_weight, error_buffer, q_start):
    c, x = lax.axis_index("c"), lax.axis_index("x")
    place = jnp.stack([x, c]).astype(jnp.int32)
    rank = q_start.shape[0]
    error = error_buffer[0]

    with jax.named_scope("exchange"):
        sub = kv_weight.shape[0] // NC
        mine = lax.dynamic_slice_in_dim(kv_weight, c * sub, sub, axis=0)
        column = jnp.stack(swaps(mine, "x", NX))
        column, packed = lax.optimization_barrier((column, pack(activations, cotangent)))
        weight = lax.all_gather(column, "z", axis=0)
        gathered = lax.all_to_all(packed, "x", 0, 0, tiled=True)
        p_own = jnp.einsum("rk,dk->rd", q_start, error, precision=HIGHEST)
        gathered, p_own = lax.optimization_barrier((gathered, p_own))
        gathered = gathered.reshape(-1, gathered.shape[2])

    with jax.named_scope("gradient"):
        part, p_part = gradient_terms(q_start, gathered)
        gradient = lax.psum_scatter(part, "z", scatter_dimension=0, tiled=True)

    with jax.named_scope("left"):
        p_part = lax.all_to_all(p_part, "z", 0, 0, tiled=True)
        p_total = tree([p_part[i] for i in range(NZ)]) * (1.0 / LOSS_SCALE) + p_own
        p_total = tree(swaps(p_total, "c", NC))
        p_total = tree(swaps(p_total, "y", NY))
        p_line = jnp.broadcast_to(p_total[None], (NZ,) + p_total.shape)
        p_line = lax.all_to_all(p_line, "z", 0, 0, tiled=True)

    with jax.named_scope("weight"):
        input_grad = project(place, cotangent, weight, swap(weight, "c", NC, 1))

    with jax.named_scope("sums"):
        keep, give = right_terms(place, input_grad[:16, :128], gathered, p_line, p_total, error)
        keep = keep + swap(give, "c", NC, 1)
        keep = tree(swaps(keep, "y", NY))
        keep = tree(swaps(keep, "x", NX))
        keep = keep + swap(keep, "z", NZ, 1)
        keep = tree([keep] + [swap(keep, "z", NZ, k) for k in (2, 4, 6)])
        other = swap(keep, "c", NC, 1)

    with jax.named_scope("finish"):
        error_next, compressed, q_next = finish(place, keep, other, p_total, gradient, error)
    return (input_grad, error_next[None], compressed, q_next)


def solution(mesh):
    fine = Mesh(mesh.devices.reshape(NY, NC, NX, NZ), ("y", "c", "x", "z"))
    dp, fsdp = ("y", "c"), ("x", "z")
    return jax.shard_map(
        local,
        mesh=fine,
        in_specs=(P(dp + fsdp, None), P(dp + fsdp, None), P(fsdp, None), P(dp, fsdp, None), P()),
        out_specs=(P(dp + fsdp, None), P(dp, fsdp, None), P(fsdp, None), P()),
        check_vma=False,
    )
```

```python
import functools

import jax
import jax.numpy as jnp
from jax import lax
from jax.experimental import pallas as pl
from jax.experimental.pallas import tpu as pltpu
from jax.sharding import Mesh, PartitionSpec as P

LOSS_SCALE = 256.0
HIGHEST = lax.Precision.HIGHEST
F32 = jnp.float32
BF16 = jnp.bfloat16
NY, NC, NX, NZ = 4, 2, 4, 8
NT = (((1,), (1,)), ((), ()))
TN = (((0,), (0,)), ((), ()))


def swap(value, axis, size, k):
    return lax.ppermute(value, axis, [(i, i ^ k) for i in range(size)])


def swaps(value, axis, size):
    return [value] + [swap(value, axis, size, k) for k in range(1, size)]


def tree(parts):
    while len(parts) > 1:
        parts = [parts[i] + parts[i + 1] for i in range(0, len(parts), 2)]
    return parts[0]


def thirds(value):
    parts = []
    for _ in range(3):
        part = value.astype(BF16)
        parts.append(part)
        value = value - part.astype(F32)
    return jnp.concatenate(parts, axis=0)


def join(value):
    rank = value.shape[0] // 3
    return value[:rank] + (value[rank:2 * rank] + value[2 * rank:])


def load_tokens(refs, rows):
    at = 0
    for ref in refs:
        rows[at:at + ref.shape[0], :] = ref[...]
        at += ref.shape[0]


def gradient_kernel(count, place, *refs):
    cots, acts = refs[:NX], refs[NX:NX + count]
    gradient, lhs, cot_rows, rows = refs[NX + count:]

    @pl.when(pl.program_id(0) == 0)
    def _():
        load_tokens(cots, cot_rows)
        lhs[...] = cot_rows[...].T

    load_tokens(acts, rows)
    gradient[0] = jnp.dot(lhs[...], rows[...], preferred_element_type=F32)


def left_kernel(count, place, q, error, *refs):
    cots, acts = refs[:NX], refs[NX:NX + count]
    left, lhs, cot_rows, rows = refs[NX + count:]
    z = pl.program_id(0)
    block = acts[0].shape[1]

    @pl.when(z == 0)
    def _():
        load_tokens(cots, cot_rows)
        q_cot = lax.dot_general(
            q[...], cot_rows[...].astype(F32), NT, precision=HIGHEST, preferred_element_type=F32
        )
        lhs[...] = thirds(q_cot)

    load_tokens(acts, rows)
    part = join(jnp.dot(lhs[...], rows[...], preferred_element_type=F32)) * (1.0 / LOSS_SCALE)
    left[:, 0] = part.reshape(NY * NC, -1, block)

    @pl.when(z == place[2])
    def _():
        own = lax.dot_general(q[...], error[...], NT, precision=HIGHEST, preferred_element_type=F32)
        left[:, 0] = left[:, 0] + own.reshape(NY * NC, -1, block)


def token_specs(activations, cots, pieces):
    block = activations.shape[1] // (NX * NZ)
    tokens, width = cots[0].shape
    specs = [pl.BlockSpec((tokens, width), lambda z, place: (0, 0))] * NX
    specs.append(pl.BlockSpec((tokens, block), lambda z, place: (0, place[0] * NZ + z)))
    specs += [pl.BlockSpec((piece.shape[0], block), lambda z, place: (0, z)) for piece in pieces]
    return specs


def gradient_terms(place, activations, cots, pieces):
    width = cots[0].shape[1]
    tokens = NX * cots[0].shape[0]
    block = activations.shape[1] // (NX * NZ)
    return pl.pallas_call(
        functools.partial(gradient_kernel, 1 + len(pieces)),
        out_shape=jax.ShapeDtypeStruct((NZ, width, block), F32),
        grid_spec=pltpu.PrefetchScalarGridSpec(
            num_scalar_prefetch=1,
            grid=(NZ,),
            in_specs=token_specs(activations, cots, pieces),
            out_specs=pl.BlockSpec((1, width, block), lambda z, place: (z, 0, 0)),
            scratch_shapes=[pltpu.VMEM(shape, BF16) for shape in ((width, tokens), (tokens, width), (tokens, block))],
        ),
        cost_estimate=pl.CostEstimate(
            flops=2 * width * tokens * block * NZ,
            bytes_accessed=(2 * tokens + 4 * width) * block * NZ,
            transcendentals=0,
        ),
        compiler_params=pltpu.CompilerParams(vmem_limit_bytes=60 * 1024 * 1024),
        name="gradient_terms",
    )(place, *cots, activations, *pieces)


def left_terms(place, q_start, error, activations, cots, pieces):
    rank, width = q_start.shape
    tokens = NX * cots[0].shape[0]
    block = activations.shape[1] // (NX * NZ)
    shares = NY * NC
    return pl.pallas_call(
        functools.partial(left_kernel, 1 + len(pieces)),
        out_shape=jax.ShapeDtypeStruct((shares, NZ, rank // shares, block), F32),
        grid_spec=pltpu.PrefetchScalarGridSpec(
            num_scalar_prefetch=1,
            grid=(NZ,),
            in_specs=[
                pl.BlockSpec((rank, width), lambda z, place: (0, 0)),
                pl.BlockSpec((block, width), lambda z, place: (0, 0)),
            ]
            + token_specs(activations, cots, pieces),
            out_specs=pl.BlockSpec((shares, 1, rank // shares, block), lambda z, place: (0, z, 0, 0)),
            scratch_shapes=[pltpu.VMEM(shape, BF16) for shape in ((3 * rank, tokens), (tokens, width), (tokens, block))],
        ),
        cost_estimate=pl.CostEstimate(
            flops=6 * rank * tokens * block * NZ,
            bytes_accessed=2 * tokens * block * NZ,
            transcendentals=0,
        ),
        compiler_params=pltpu.CompilerParams(vmem_limit_bytes=60 * 1024 * 1024),
        name="left_terms",
    )(place, q_start, error, *cots, activations, *pieces)


def project_kernel(place, cot, own, other, out, rows, arrived):
    sub = own.shape[2]
    block = NC * sub

    def fetch(k, c):
        start = pl.multiple_of((place[1] ^ c) * sub, sub)
        return pltpu.make_async_copy(
            (own, other)[c].at[:, k], rows.at[k, :, pl.ds(start, sub), :], arrived.at[NC * k + c]
        )

    @pl.when(pl.program_id(0) == 0)
    def _():
        for k in range(NX):
            for c in range(NC):
                fetch(k, c).start()

    for k in range(NX):
        @pl.when(pl.program_id(0) == k)
        def _():
            for c in range(NC):
                fetch(k, c).wait()
            for z in range(NZ):
                out[:, z * block:(z + 1) * block] = lax.dot_general(
                    cot[...], rows[k, z], NT, preferred_element_type=F32
                ).astype(BF16)


def project(place, cot, own, other):
    tokens, width = cot.shape
    sub = own.shape[2]
    columns = NZ * NC * sub
    return pl.pallas_call(
        project_kernel,
        out_shape=jax.ShapeDtypeStruct((tokens, NX * columns), BF16),
        grid_spec=pltpu.PrefetchScalarGridSpec(
            num_scalar_prefetch=1,
            grid=(NX,),
            in_specs=[pl.BlockSpec((tokens, width), lambda k, place: (0, 0))]
            + [pl.BlockSpec(memory_space=pltpu.HBM)] * 2,
            out_specs=pl.BlockSpec((tokens, columns), lambda k, place: (0, k ^ place[0])),
            scratch_shapes=[pltpu.VMEM((NX, NZ, NC * sub, width), BF16), pltpu.SemaphoreType.DMA((NC * NX,))],
        ),
        cost_estimate=pl.CostEstimate(
            flops=2 * tokens * width * NX * columns,
            bytes_accessed=2 * (tokens + width) * NX * columns,
            transcendentals=0,
        ),
        compiler_params=pltpu.CompilerParams(vmem_limit_bytes=62_000_000),
        name="project",
    )(place, cot, own, other)


def right_kernel(place, _, gradient, error, p_total, merged_out, keep, give):
    half = keep.shape[0]
    merged = gradient[0].T * (1.0 / LOSS_SCALE) + error[...]
    merged_out[...] = merged
    p = p_total[...]
    right = jnp.dot(p, merged, precision=HIGHEST, preferred_element_type=F32)
    gram = lax.dot_general(p, p, NT, precision=HIGHEST, preferred_element_type=F32) * (1.0 / (NY * NC))
    sums = jnp.concatenate([right, gram], axis=1)
    first = place[1] == 0
    keep[...] = jnp.where(first, sums[:half], sums[half:])
    give[...] = jnp.where(first, sums[half:], sums[:half])


def right_terms(place, after, gradient, error, p_total):
    rank, width = p_total.shape[0], error.shape[1]
    half = jax.ShapeDtypeStruct((rank // NC, width + rank), F32)
    return pl.pallas_call(
        right_kernel,
        out_shape=(jax.ShapeDtypeStruct(error.shape, F32), half, half),
        in_specs=[pl.BlockSpec(memory_space=pltpu.SMEM), pl.BlockSpec(memory_space=pltpu.HBM)]
        + [pl.BlockSpec(memory_space=pltpu.VMEM)] * 3,
        compiler_params=pltpu.CompilerParams(vmem_limit_bytes=32 * 1024 * 1024),
        name="right_terms",
    )(place, after, gradient, error, p_total)


def eliminate(gram):
    rank = gram.shape[0]
    group = 4
    row = lax.broadcasted_iota(jnp.int32, (rank, 2 * rank), 0)
    col = lax.broadcasted_iota(jnp.int32, (rank, 2 * rank), 1)
    work = jnp.where(col == row + rank, 1.0, jnp.concatenate([gram, jnp.zeros_like(gram)], axis=1))
    scale = jnp.zeros_like(work)
    for base in range(0, rank, group):
        at = [base + j for j in range(group)]
        cols = [jnp.broadcast_to(work[:, k:k + 1], work.shape) for k in at]
        rows = [work[k:k + 1, :] for k in at]
        for j, k in enumerate(at):
            pivot = cols[j][k:k + 1, :]
            ratio = jnp.where(row > k, cols[j] * (1.0 / pivot), 0.0)
            scale = jnp.where(row == k, lax.rsqrt(pivot), scale)
            for i in range(j + 1, group):
                cols[i] = cols[i] - ratio * cols[i][k:k + 1, :]
                rows[i] = rows[i] - ratio[at[i]:at[i] + 1, :] * rows[j]
            work = work - ratio * rows[j]
    return (work * scale)[:, rank:]


def finish_kernel(place, mine, other, p_total, merged, error_out, compressed_out, q_out):
    width = merged.shape[1]
    first = place[1] == 0
    sums = jnp.concatenate([jnp.where(first, mine[...], other[...]), jnp.where(first, other[...], mine[...])], axis=0)
    inverse = eliminate(sums[:, width:])
    q_next = jnp.dot(inverse, sums[:, :width], precision=HIGHEST, preferred_element_type=F32) * (1.0 / (NY * NC))
    p_basis = jnp.dot(inverse, p_total[...], precision=HIGHEST, preferred_element_type=F32)
    compressed = lax.dot_general(p_basis, q_next, TN, precision=HIGHEST, preferred_element_type=F32)
    q_out[...] = q_next
    compressed_out[...] = compressed
    error_out[...] = merged[...] - compressed


def finish(place, mine, other, p_total, merged):
    rank = p_total.shape[0]
    return pl.pallas_call(
        finish_kernel,
        out_shape=(
            jax.ShapeDtypeStruct(merged.shape, F32),
            jax.ShapeDtypeStruct(merged.shape, F32),
            jax.ShapeDtypeStruct((rank, merged.shape[1]), F32),
        ),
        in_specs=[pl.BlockSpec(memory_space=pltpu.SMEM)] + [pl.BlockSpec(memory_space=pltpu.VMEM)] * 4,
        compiler_params=pltpu.CompilerParams(vmem_limit_bytes=32 * 1024 * 1024),
        name="finish",
    )(place, mine, other, p_total, merged)


def local(activations, cotangent, kv_weight, error_buffer, q_start):
    c, x, z = (lax.axis_index(a) for a in "cxz")
    place = jnp.stack([x, c, z]).astype(jnp.int32)
    error = error_buffer[0]
    tokens = cotangent.shape[0]
    columns = activations.shape[1] // NX

    with jax.named_scope("exchange"):
        cots, pieces = [cotangent], []
        for k in (2, 1, 3):
            cots.append(swap(cotangent, "x", NX, k))
            for h in range(2):
                piece = lax.dynamic_slice(activations, (h * (tokens // 2), (x ^ k) * columns), (tokens // 2, columns))
                pieces.append(swap(piece, "x", NX, k))
        sub = kv_weight.shape[0] // NC
        mine = lax.dynamic_slice_in_dim(kv_weight, c * sub, sub, axis=0)
        column = jnp.stack(swaps(mine, "x", NX))
        weight = lax.all_gather(column, "z", axis=0)

    with jax.named_scope("gradient"):
        part = gradient_terms(place, activations, cots, pieces)
        part, cots, pieces = lax.optimization_barrier((part, cots, pieces))
        gradient = lax.psum_scatter(part, "z", scatter_dimension=0, tiled=True)

    with jax.named_scope("left"):
        left = left_terms(place, q_start, error, activations, cots, pieces)
        left = tree(list(lax.all_to_all(left, ("y", "c"), 0, 0, tiled=True)))
        left = tree(list(lax.all_to_all(left, "z", 0, 0, tiled=True)))
        left = jnp.broadcast_to(left[None], (NY * NC,) + left.shape)
        p_total = lax.all_to_all(left, ("y", "c"), 0, 0, tiled=True).reshape(q_start.shape[0], -1)

    with jax.named_scope("weight"):
        input_grad = project(place, cotangent, weight, swap(weight, "c", NC, 1))

    with jax.named_scope("sums"):
        merged, keep, give = right_terms(place, input_grad[:16, :128], gradient, error, p_total)
        keep = keep + swap(give, "c", NC, 1)
        keep = tree(swaps(keep, "y", NY))
        keep = tree(swaps(keep, "x", NX))
        keep = keep + swap(keep, "z", NZ, 1)
        keep = tree([keep] + [swap(keep, "z", NZ, k) for k in (2, 4, 6)])
        other = swap(keep, "c", NC, 1)

    with jax.named_scope("finish"):
        error_next, compressed, q_next = finish(place, keep, other, p_total, merged)
    return (input_grad, error_next[None], compressed, q_next)


def solution(mesh):
    fine = Mesh(mesh.devices.reshape(NY, NC, NX, NZ), ("y", "c", "x", "z"))
    dp, fsdp = ("y", "c"), ("x", "z")
    return jax.shard_map(
        local,
        mesh=fine,
        in_specs=(P(dp + fsdp, None), P(dp + fsdp, None), P(fsdp, None), P(dp, fsdp, None), P()),
        out_specs=(P(dp + fsdp, None), P(dp, fsdp, None), P(fsdp, None), P()),
        check_vma=False,
    )
```

```python
import functools

import jax
import jax.numpy as jnp
from jax import lax
from jax.experimental import pallas as pl
from jax.experimental.pallas import tpu as pltpu
from jax.sharding import Mesh, PartitionSpec as P

LOSS_SCALE = 256.0
HIGHEST = lax.Precision.HIGHEST
F32 = jnp.float32
BF16 = jnp.bfloat16
NY, NC, NX, NZ = 4, 2, 4, 8
NT = (((1,), (1,)), ((), ()))
TN = (((0,), (0,)), ((), ()))


def swap(value, axis, size, k):
    return lax.ppermute(value, axis, [(i, i ^ k) for i in range(size)])


def swaps(value, axis, size):
    return [value] + [swap(value, axis, size, k) for k in range(1, size)]


def tree(parts):
    while len(parts) > 1:
        parts = [parts[i] + parts[i + 1] for i in range(0, len(parts), 2)]
    return parts[0]


def thirds(value):
    parts = []
    for _ in range(3):
        part = value.astype(BF16)
        parts.append(part)
        value = value - part.astype(F32)
    return jnp.concatenate(parts, axis=0)


def join(value):
    rank = value.shape[0] // 3
    return value[:rank] + (value[rank:2 * rank] + value[2 * rank:])


PARTNERS = (2, 1, 3)


def pack_kernel(place, act, cot, *outs):
    rows, columns = outs[0].shape[0], act.shape[1]
    for j in range(len(PARTNERS)):
        @pl.when(pl.program_id(0) == j)
        def _():
            for h in range(2):
                outs[2 * j + h][:, :columns] = act[h * rows:(h + 1) * rows, :]
                outs[2 * j + h][:, columns:] = cot[h * rows:(h + 1) * rows, :]


def pack(place, activations, cotangent):
    tokens, width = cotangent.shape
    columns = activations.shape[1] // NX
    shape = (tokens // 2, columns + width)
    return pl.pallas_call(
        pack_kernel,
        out_shape=(jax.ShapeDtypeStruct(shape, BF16),) * (2 * len(PARTNERS)),
        grid_spec=pltpu.PrefetchScalarGridSpec(
            num_scalar_prefetch=1,
            grid=(len(PARTNERS),),
            in_specs=[
                pl.BlockSpec((tokens, columns), lambda j, place: (0, place[3 + j])),
                pl.BlockSpec((tokens, width), lambda j, place: (0, 0)),
            ],
            out_specs=[pl.BlockSpec(shape, lambda j, place: (0, 0))] * (2 * len(PARTNERS)),
        ),
        cost_estimate=pl.CostEstimate(flops=0, bytes_accessed=8 * tokens * columns * 2, transcendentals=0),
        compiler_params=pltpu.CompilerParams(vmem_limit_bytes=60 * 1024 * 1024),
        name="pack",
    )(place, activations, cotangent)


def load_tokens(refs, rows):
    at = 0
    for ref in refs:
        rows[at:at + ref.shape[0], :] = ref[...]
        at += ref.shape[0]


def gradient_kernel(count, place, *refs):
    cots, acts = refs[:count], refs[count:2 * count]
    gradient, lhs, cot_rows, rows = refs[2 * count:]

    @pl.when(pl.program_id(0) == 0)
    def _():
        load_tokens(cots, cot_rows)
        lhs[...] = cot_rows[...].T

    load_tokens(acts, rows)
    block = gradient.shape[2]
    for i in range(gradient.shape[0]):
        gradient[i] = jnp.dot(lhs[...], rows[:, i * block:(i + 1) * block], preferred_element_type=F32)


def left_kernel(count, place, q, error, *refs):
    cots, acts = refs[:count], refs[count:2 * count]
    left, lhs, cot_rows, rows = refs[2 * count:]
    z = pl.program_id(0)
    block = acts[0].shape[1]

    @pl.when(z == 0)
    def _():
        load_tokens(cots, cot_rows)
        q_cot = lax.dot_general(
            q[...], cot_rows[...].astype(F32), NT, precision=HIGHEST, preferred_element_type=F32
        )
        lhs[...] = thirds(q_cot)

    load_tokens(acts, rows)
    part = join(jnp.dot(lhs[...], rows[...], preferred_element_type=F32)) * (1.0 / LOSS_SCALE)
    left[:, 0] = part.reshape(NY * NC, -1, block)

    @pl.when(z == place[2])
    def _():
        own = lax.dot_general(q[...], error[...], NT, precision=HIGHEST, preferred_element_type=F32)
        left[:, 0] = left[:, 0] + own.reshape(NY * NC, -1, block)


def token_specs(activations, cotangent, pieces, steps):
    tokens, width = cotangent.shape
    block = activations.shape[1] // (NX * steps)
    part = pieces[0].shape[0]
    last = block * steps // width
    specs = [pl.BlockSpec((tokens, width), lambda i, place: (0, 0))]
    specs += [pl.BlockSpec((part, width), lambda i, place: (0, last))] * len(pieces)
    specs.append(pl.BlockSpec((tokens, block), lambda i, place: (0, place[0] * steps + i)))
    specs += [pl.BlockSpec((part, block), lambda i, place: (0, i))] * len(pieces)
    return specs


def gradient_terms(place, activations, cotangent, pieces):
    width = cotangent.shape[1]
    tokens = NX * cotangent.shape[0]
    columns = activations.shape[1] // NX
    steps = 4
    return pl.pallas_call(
        functools.partial(gradient_kernel, 1 + len(pieces)),
        out_shape=jax.ShapeDtypeStruct((NZ, width, columns // NZ), F32),
        grid_spec=pltpu.PrefetchScalarGridSpec(
            num_scalar_prefetch=1,
            grid=(steps,),
            in_specs=token_specs(activations, cotangent, pieces, steps),
            out_specs=pl.BlockSpec((NZ // steps, width, columns // NZ), lambda i, place: (i, 0, 0)),
            scratch_shapes=[
                pltpu.VMEM(shape, BF16) for shape in ((width, tokens), (tokens, width), (tokens, columns // steps))
            ],
        ),
        cost_estimate=pl.CostEstimate(
            flops=2 * width * tokens * columns,
            bytes_accessed=(2 * tokens + 4 * width) * columns,
            transcendentals=0,
        ),
        compiler_params=pltpu.CompilerParams(vmem_limit_bytes=60 * 1024 * 1024),
        name="gradient_terms",
    )(place, cotangent, *pieces, activations, *pieces)


def left_terms(place, q_start, error, activations, cotangent, pieces):
    rank, width = q_start.shape
    tokens = NX * cotangent.shape[0]
    block = activations.shape[1] // (NX * NZ)
    shares = NY * NC
    return pl.pallas_call(
        functools.partial(left_kernel, 1 + len(pieces)),
        out_shape=jax.ShapeDtypeStruct((shares, NZ, rank // shares, block), F32),
        grid_spec=pltpu.PrefetchScalarGridSpec(
            num_scalar_prefetch=1,
            grid=(NZ,),
            in_specs=[
                pl.BlockSpec((rank, width), lambda z, place: (0, 0)),
                pl.BlockSpec((block, width), lambda z, place: (0, 0)),
            ]
            + token_specs(activations, cotangent, pieces, NZ),
            out_specs=pl.BlockSpec((shares, 1, rank // shares, block), lambda z, place: (0, z, 0, 0)),
            scratch_shapes=[pltpu.VMEM(shape, BF16) for shape in ((3 * rank, tokens), (tokens, width), (tokens, block))],
        ),
        cost_estimate=pl.CostEstimate(
            flops=6 * rank * tokens * block * NZ,
            bytes_accessed=2 * tokens * block * NZ,
            transcendentals=0,
        ),
        compiler_params=pltpu.CompilerParams(vmem_limit_bytes=60 * 1024 * 1024),
        name="left_terms",
    )(place, q_start, error, cotangent, *pieces, activations, *pieces)


def project_kernel(place, cot, own, other, out, rows, arrived):
    sub = own.shape[2]
    block = NC * sub

    def fetch(k, c):
        start = pl.multiple_of((place[1] ^ c) * sub, sub)
        return pltpu.make_async_copy(
            (own, other)[c].at[:, k], rows.at[k, :, pl.ds(start, sub), :], arrived.at[NC * k + c]
        )

    @pl.when(pl.program_id(0) == 0)
    def _():
        for k in range(NX):
            for c in range(NC):
                fetch(k, c).start()

    for k in range(NX):
        @pl.when(pl.program_id(0) == k)
        def _():
            for c in range(NC):
                fetch(k, c).wait()
            for z in range(NZ):
                out[:, z * block:(z + 1) * block] = lax.dot_general(
                    cot[...], rows[k, z], NT, preferred_element_type=F32
                ).astype(BF16)


def project(place, cot, own, other):
    tokens, width = cot.shape
    sub = own.shape[2]
    columns = NZ * NC * sub
    return pl.pallas_call(
        project_kernel,
        out_shape=jax.ShapeDtypeStruct((tokens, NX * columns), BF16),
        grid_spec=pltpu.PrefetchScalarGridSpec(
            num_scalar_prefetch=1,
            grid=(NX,),
            in_specs=[pl.BlockSpec((tokens, width), lambda k, place: (0, 0))]
            + [pl.BlockSpec(memory_space=pltpu.HBM)] * 2,
            out_specs=pl.BlockSpec((tokens, columns), lambda k, place: (0, k ^ place[0])),
            scratch_shapes=[pltpu.VMEM((NX, NZ, NC * sub, width), BF16), pltpu.SemaphoreType.DMA((NC * NX,))],
        ),
        cost_estimate=pl.CostEstimate(
            flops=2 * tokens * width * NX * columns,
            bytes_accessed=2 * (tokens + width) * NX * columns,
            transcendentals=0,
        ),
        compiler_params=pltpu.CompilerParams(vmem_limit_bytes=62_000_000),
        name="project",
    )(place, cot, own, other)


def right_kernel(place, _, gradient, error, p_total, merged_out, keep, give):
    half = keep.shape[0]
    merged = gradient[0].T * (1.0 / LOSS_SCALE) + error[...]
    merged_out[...] = merged
    p = p_total[...]
    right = jnp.dot(p, merged, precision=HIGHEST, preferred_element_type=F32)
    gram = lax.dot_general(p, p, NT, precision=HIGHEST, preferred_element_type=F32) * (1.0 / (NY * NC))
    sums = jnp.concatenate([right, gram], axis=1)
    first = place[1] == 0
    keep[...] = jnp.where(first, sums[:half], sums[half:])
    give[...] = jnp.where(first, sums[half:], sums[:half])


def right_terms(place, after, gradient, error, p_total):
    rank, width = p_total.shape[0], error.shape[1]
    half = jax.ShapeDtypeStruct((rank // NC, width + rank), F32)
    return pl.pallas_call(
        right_kernel,
        out_shape=(jax.ShapeDtypeStruct(error.shape, F32), half, half),
        in_specs=[pl.BlockSpec(memory_space=pltpu.SMEM), pl.BlockSpec(memory_space=pltpu.HBM)]
        + [pl.BlockSpec(memory_space=pltpu.VMEM)] * 3,
        compiler_params=pltpu.CompilerParams(vmem_limit_bytes=32 * 1024 * 1024),
        name="right_terms",
    )(place, after, gradient, error, p_total)


def eliminate(gram):
    rank = gram.shape[0]
    group = 4
    row = lax.broadcasted_iota(jnp.int32, (rank, 2 * rank), 0)
    col = lax.broadcasted_iota(jnp.int32, (rank, 2 * rank), 1)
    work = jnp.where(col == row + rank, 1.0, jnp.concatenate([gram, jnp.zeros_like(gram)], axis=1))
    scale = jnp.zeros_like(work)
    for base in range(0, rank, group):
        at = [base + j for j in range(group)]
        cols = [jnp.broadcast_to(work[:, k:k + 1], work.shape) for k in at]
        rows = [work[k:k + 1, :] for k in at]
        for j, k in enumerate(at):
            pivot = cols[j][k:k + 1, :]
            ratio = jnp.where(row > k, cols[j] * (1.0 / pivot), 0.0)
            scale = jnp.where(row == k, lax.rsqrt(pivot), scale)
            for i in range(j + 1, group):
                cols[i] = cols[i] - ratio * cols[i][k:k + 1, :]
                rows[i] = rows[i] - ratio[at[i]:at[i] + 1, :] * rows[j]
            work = work - ratio * rows[j]
    return (work * scale)[:, rank:]


def finish_kernel(place, mine, other, p_total, merged, error_out, compressed_out, q_out):
    width = merged.shape[1]
    first = place[1] == 0
    sums = jnp.concatenate([jnp.where(first, mine[...], other[...]), jnp.where(first, other[...], mine[...])], axis=0)
    inverse = eliminate(sums[:, width:])
    q_next = jnp.dot(inverse, sums[:, :width], precision=HIGHEST, preferred_element_type=F32) * (1.0 / (NY * NC))
    p_basis = jnp.dot(inverse, p_total[...], precision=HIGHEST, preferred_element_type=F32)
    compressed = lax.dot_general(p_basis, q_next, TN, precision=HIGHEST, preferred_element_type=F32)
    q_out[...] = q_next
    compressed_out[...] = compressed
    error_out[...] = merged[...] - compressed


def finish(place, mine, other, p_total, merged):
    rank = p_total.shape[0]
    return pl.pallas_call(
        finish_kernel,
        out_shape=(
            jax.ShapeDtypeStruct(merged.shape, F32),
            jax.ShapeDtypeStruct(merged.shape, F32),
            jax.ShapeDtypeStruct((rank, merged.shape[1]), F32),
        ),
        in_specs=[pl.BlockSpec(memory_space=pltpu.SMEM)] + [pl.BlockSpec(memory_space=pltpu.VMEM)] * 4,
        compiler_params=pltpu.CompilerParams(vmem_limit_bytes=32 * 1024 * 1024),
        name="finish",
    )(place, mine, other, p_total, merged)


def local(activations, cotangent, kv_weight, error_buffer, q_start):
    c, x, z = (lax.axis_index(a) for a in "cxz")
    place = jnp.stack([x, c, z] + [x ^ k for k in PARTNERS]).astype(jnp.int32)
    error = error_buffer[0]

    with jax.named_scope("exchange"):
        sub = kv_weight.shape[0] // NC
        mine = lax.dynamic_slice_in_dim(kv_weight, c * sub, sub, axis=0)
        column = jnp.stack(swaps(mine, "x", NX))
        packed = pack(place, activations, cotangent)
        column, packed = lax.optimization_barrier((column, packed))
        weight = lax.all_gather(column, "z", axis=0)
        pieces = [swap(packed[i], "x", NX, PARTNERS[i // 2]) for i in (0, 2, 4, 1, 3, 5)]

    with jax.named_scope("gradient"):
        part = gradient_terms(place, activations, cotangent, pieces)
        part, pieces = lax.optimization_barrier((part, pieces))
        gradient = lax.psum_scatter(part, "z", scatter_dimension=0, tiled=True)

    with jax.named_scope("left"):
        left = left_terms(place, q_start, error, activations, cotangent, pieces)
        left = tree(list(lax.all_to_all(left, ("y", "c"), 0, 0, tiled=True)))
        left = tree(list(lax.all_to_all(left, "z", 0, 0, tiled=True)))
        left = jnp.broadcast_to(left[None], (NY * NC,) + left.shape)
        p_total = lax.all_to_all(left, ("y", "c"), 0, 0, tiled=True).reshape(q_start.shape[0], -1)

    with jax.named_scope("weight"):
        input_grad = project(place, cotangent, weight, swap(weight, "c", NC, 1))

    with jax.named_scope("sums"):
        merged, keep, give = right_terms(place, input_grad[:16, :128], gradient, error, p_total)
        keep = keep + swap(give, "c", NC, 1)
        keep = tree(swaps(keep, "y", NY))
        keep = tree(swaps(keep, "x", NX))
        keep = keep + swap(keep, "z", NZ, 1)
        keep = tree([keep] + [swap(keep, "z", NZ, k) for k in (2, 4, 6)])
        other = swap(keep, "c", NC, 1)

    with jax.named_scope("finish"):
        error_next, compressed, q_next = finish(place, keep, other, p_total, merged)
    return (input_grad, error_next[None], compressed, q_next)


def solution(mesh):
    fine = Mesh(mesh.devices.reshape(NY, NC, NX, NZ), ("y", "c", "x", "z"))
    dp, fsdp = ("y", "c"), ("x", "z")
    return jax.shard_map(
        local,
        mesh=fine,
        in_specs=(P(dp + fsdp, None), P(dp + fsdp, None), P(fsdp, None), P(dp, fsdp, None), P()),
        out_specs=(P(dp + fsdp, None), P(dp, fsdp, None), P(fsdp, None), P()),
        check_vma=False,
    )
```

```python
import functools

import jax
import jax.numpy as jnp
from jax import lax
from jax.experimental import pallas as pl
from jax.experimental.pallas import tpu as pltpu
from jax.sharding import Mesh, PartitionSpec as P

LOSS_SCALE = 256.0
HIGHEST = lax.Precision.HIGHEST
F32 = jnp.float32
BF16 = jnp.bfloat16
NY, NC, NX, NZ = 4, 2, 4, 8
NT = (((1,), (1,)), ((), ()))
TN = (((0,), (0,)), ((), ()))


def swap(value, axis, size, k):
    return lax.ppermute(value, axis, [(i, i ^ k) for i in range(size)])


def swaps(value, axis, size):
    return [value] + [swap(value, axis, size, k) for k in range(1, size)]


def tree(parts):
    while len(parts) > 1:
        parts = [parts[i] + parts[i + 1] for i in range(0, len(parts), 2)]
    return parts[0]


def thirds(value):
    parts = []
    for _ in range(3):
        part = value.astype(BF16)
        parts.append(part)
        value = value - part.astype(F32)
    return jnp.concatenate(parts, axis=0)


def join(value):
    rank = value.shape[0] // 3
    return value[:rank] + (value[rank:2 * rank] + value[2 * rank:])


PARTNERS = (2, 1, 3)


def pack_kernel(place, act, cot, *refs):
    outs, arrived = refs[:-1], refs[-1]
    rows = outs[0].shape[0]
    columns = act.shape[1] // NX
    copies = []
    for i, out in enumerate(outs):
        here = pl.ds((i % 2) * rows, rows)
        start = pl.multiple_of(place[3 + i // 2] * columns, columns)
        copies.append((act.at[here, pl.ds(start, columns)], out.at[:, pl.ds(0, columns)]))
        copies.append((cot.at[here, :], out.at[:, pl.ds(columns, cot.shape[1])]))
    copies = [pltpu.make_async_copy(src, dst, arrived.at[i]) for i, (src, dst) in enumerate(copies)]
    for copy in copies:
        copy.start()
    for copy in copies:
        copy.wait()


def pack(place, activations, cotangent):
    tokens, width = cotangent.shape
    count = 2 * len(PARTNERS)
    shape = jax.ShapeDtypeStruct((tokens // 2, activations.shape[1] // NX + width), BF16)
    return pl.pallas_call(
        pack_kernel,
        out_shape=(shape,) * count,
        in_specs=[pl.BlockSpec(memory_space=pltpu.SMEM)] + [pl.BlockSpec(memory_space=pltpu.HBM)] * 2,
        out_specs=[pl.BlockSpec(memory_space=pltpu.VMEM)] * count,
        scratch_shapes=[pltpu.SemaphoreType.DMA((2 * count,))],
        cost_estimate=pl.CostEstimate(flops=0, bytes_accessed=2 * activations.size, transcendentals=0),
        compiler_params=pltpu.CompilerParams(vmem_limit_bytes=46 * 1024 * 1024),
        name="pack",
    )(place, activations, cotangent)


def load_tokens(refs, rows):
    at = 0
    for ref in refs:
        rows[at:at + ref.shape[0], :] = ref[...]
        at += ref.shape[0]


def gradient_kernel(count, place, *refs):
    cots, acts = refs[:count], refs[count:2 * count]
    gradient, lhs, cot_rows, rows = refs[2 * count:]

    @pl.when(pl.program_id(0) == 0)
    def _():
        load_tokens(cots, cot_rows)
        lhs[...] = cot_rows[...].T

    load_tokens(acts, rows)
    block = gradient.shape[2]
    for i in range(gradient.shape[0]):
        gradient[i] = jnp.dot(lhs[...], rows[:, i * block:(i + 1) * block], preferred_element_type=F32)


def left_kernel(count, place, q, error, *refs):
    cots, acts = refs[:count], refs[count:2 * count]
    left, lhs, cot_rows, rows = refs[2 * count:]
    z = pl.program_id(0)
    block = acts[0].shape[1]

    @pl.when(z == 0)
    def _():
        load_tokens(cots, cot_rows)
        q_cot = lax.dot_general(
            q[...], cot_rows[...].astype(F32), NT, precision=HIGHEST, preferred_element_type=F32
        )
        lhs[...] = thirds(q_cot)

    load_tokens(acts, rows)
    part = join(jnp.dot(lhs[...], rows[...], preferred_element_type=F32)) * (1.0 / LOSS_SCALE)
    left[:, 0] = part.reshape(NY * NC, -1, block)

    @pl.when(z == place[2])
    def _():
        own = lax.dot_general(q[...], error[...], NT, precision=HIGHEST, preferred_element_type=F32)
        left[:, 0] = left[:, 0] + own.reshape(NY * NC, -1, block)


def token_specs(activations, cotangent, pieces, steps):
    tokens, width = cotangent.shape
    block = activations.shape[1] // (NX * steps)
    part = pieces[0].shape[0]
    last = block * steps // width
    specs = [pl.BlockSpec((tokens, width), lambda i, place: (0, 0))]
    specs += [pl.BlockSpec((part, width), lambda i, place: (0, last))] * len(pieces)
    specs.append(pl.BlockSpec((tokens, block), lambda i, place: (0, place[0] * steps + i)))
    specs += [pl.BlockSpec((part, block), lambda i, place: (0, i))] * len(pieces)
    return specs


def gradient_terms(place, activations, cotangent, pieces):
    width = cotangent.shape[1]
    tokens = NX * cotangent.shape[0]
    columns = activations.shape[1] // NX
    steps = 4
    return pl.pallas_call(
        functools.partial(gradient_kernel, 1 + len(pieces)),
        out_shape=jax.ShapeDtypeStruct((NZ, width, columns // NZ), F32),
        grid_spec=pltpu.PrefetchScalarGridSpec(
            num_scalar_prefetch=1,
            grid=(steps,),
            in_specs=token_specs(activations, cotangent, pieces, steps),
            out_specs=pl.BlockSpec((NZ // steps, width, columns // NZ), lambda i, place: (i, 0, 0)),
            scratch_shapes=[
                pltpu.VMEM(shape, BF16) for shape in ((width, tokens), (tokens, width), (tokens, columns // steps))
            ],
        ),
        cost_estimate=pl.CostEstimate(
            flops=2 * width * tokens * columns,
            bytes_accessed=(2 * tokens + 4 * width) * columns,
            transcendentals=0,
        ),
        compiler_params=pltpu.CompilerParams(vmem_limit_bytes=52 * 1024 * 1024),
        name="gradient_terms",
    )(place, cotangent, *pieces, activations, *pieces)


def left_terms(place, q_start, error, activations, cotangent, pieces):
    rank, width = q_start.shape
    tokens = NX * cotangent.shape[0]
    block = activations.shape[1] // (NX * NZ)
    shares = NY * NC
    return pl.pallas_call(
        functools.partial(left_kernel, 1 + len(pieces)),
        out_shape=jax.ShapeDtypeStruct((shares, NZ, rank // shares, block), F32),
        grid_spec=pltpu.PrefetchScalarGridSpec(
            num_scalar_prefetch=1,
            grid=(NZ,),
            in_specs=[
                pl.BlockSpec((rank, width), lambda z, place: (0, 0)),
                pl.BlockSpec((block, width), lambda z, place: (0, 0)),
            ]
            + token_specs(activations, cotangent, pieces, NZ),
            out_specs=pl.BlockSpec((shares, 1, rank // shares, block), lambda z, place: (0, z, 0, 0)),
            scratch_shapes=[pltpu.VMEM(shape, BF16) for shape in ((3 * rank, tokens), (tokens, width), (tokens, block))],
        ),
        cost_estimate=pl.CostEstimate(
            flops=6 * rank * tokens * block * NZ,
            bytes_accessed=2 * tokens * block * NZ,
            transcendentals=0,
        ),
        compiler_params=pltpu.CompilerParams(vmem_limit_bytes=52 * 1024 * 1024),
        name="left_terms",
    )(place, q_start, error, cotangent, *pieces, activations, *pieces)


def project_kernel(place, cot, own, other, out, rows, arrived):
    sub = own.shape[2]
    block = NC * sub

    def fetch(k, c):
        start = pl.multiple_of((place[1] ^ c) * sub, sub)
        return pltpu.make_async_copy(
            (own, other)[c].at[:, k], rows.at[k, :, pl.ds(start, sub), :], arrived.at[NC * k + c]
        )

    @pl.when(pl.program_id(0) == 0)
    def _():
        for k in range(NX):
            for c in range(NC):
                fetch(k, c).start()

    for k in range(NX):
        @pl.when(pl.program_id(0) == k)
        def _():
            for c in range(NC):
                fetch(k, c).wait()
            for z in range(NZ):
                out[:, z * block:(z + 1) * block] = lax.dot_general(
                    cot[...], rows[k, z], NT, preferred_element_type=F32
                ).astype(BF16)


def project(place, cot, own, other):
    tokens, width = cot.shape
    sub = own.shape[2]
    columns = NZ * NC * sub
    return pl.pallas_call(
        project_kernel,
        out_shape=jax.ShapeDtypeStruct((tokens, NX * columns), BF16),
        grid_spec=pltpu.PrefetchScalarGridSpec(
            num_scalar_prefetch=1,
            grid=(NX,),
            in_specs=[pl.BlockSpec((tokens, width), lambda k, place: (0, 0))]
            + [pl.BlockSpec(memory_space=pltpu.HBM)] * 2,
            out_specs=pl.BlockSpec((tokens, columns), lambda k, place: (0, k ^ place[0])),
            scratch_shapes=[pltpu.VMEM((NX, NZ, NC * sub, width), BF16), pltpu.SemaphoreType.DMA((NC * NX,))],
        ),
        cost_estimate=pl.CostEstimate(
            flops=2 * tokens * width * NX * columns,
            bytes_accessed=2 * (tokens + width) * NX * columns,
            transcendentals=0,
        ),
        compiler_params=pltpu.CompilerParams(vmem_limit_bytes=62_000_000),
        name="project",
    )(place, cot, own, other)


def right_kernel(place, _, gradient, error, p_total, merged_out, keep, give):
    half = keep.shape[0]
    merged = gradient[0].T * (1.0 / LOSS_SCALE) + error[...]
    merged_out[...] = merged
    p = p_total[...]
    right = jnp.dot(p, merged, precision=HIGHEST, preferred_element_type=F32)
    gram = lax.dot_general(p, p, NT, precision=HIGHEST, preferred_element_type=F32) * (1.0 / (NY * NC))
    sums = jnp.concatenate([right, gram], axis=1)
    first = place[1] == 0
    keep[...] = jnp.where(first, sums[:half], sums[half:])
    give[...] = jnp.where(first, sums[half:], sums[:half])


def right_terms(place, after, gradient, error, p_total):
    rank, width = p_total.shape[0], error.shape[1]
    half = jax.ShapeDtypeStruct((rank // NC, width + rank), F32)
    return pl.pallas_call(
        right_kernel,
        out_shape=(jax.ShapeDtypeStruct(error.shape, F32), half, half),
        in_specs=[pl.BlockSpec(memory_space=pltpu.SMEM), pl.BlockSpec(memory_space=pltpu.HBM)]
        + [pl.BlockSpec(memory_space=pltpu.VMEM)] * 3,
        compiler_params=pltpu.CompilerParams(vmem_limit_bytes=32 * 1024 * 1024),
        name="right_terms",
    )(place, after, gradient, error, p_total)


def eliminate(gram):
    rank = gram.shape[0]
    group = 4
    row = lax.broadcasted_iota(jnp.int32, (rank, 2 * rank), 0)
    col = lax.broadcasted_iota(jnp.int32, (rank, 2 * rank), 1)
    work = jnp.where(col == row + rank, 1.0, jnp.concatenate([gram, jnp.zeros_like(gram)], axis=1))
    scale = jnp.zeros_like(work)
    for base in range(0, rank, group):
        at = [base + j for j in range(group)]
        cols = [jnp.broadcast_to(work[:, k:k + 1], work.shape) for k in at]
        rows = [work[k:k + 1, :] for k in at]
        for j, k in enumerate(at):
            pivot = cols[j][k:k + 1, :]
            ratio = jnp.where(row > k, cols[j] * (1.0 / pivot), 0.0)
            scale = jnp.where(row == k, lax.rsqrt(pivot), scale)
            for i in range(j + 1, group):
                cols[i] = cols[i] - ratio * cols[i][k:k + 1, :]
                rows[i] = rows[i] - ratio[at[i]:at[i] + 1, :] * rows[j]
            work = work - ratio * rows[j]
    return (work * scale)[:, rank:]


def finish_kernel(place, mine, other, p_total, merged, error_out, compressed_out, q_out):
    width = merged.shape[1]
    first = place[1] == 0
    sums = jnp.concatenate([jnp.where(first, mine[...], other[...]), jnp.where(first, other[...], mine[...])], axis=0)
    inverse = eliminate(sums[:, width:])
    q_next = jnp.dot(inverse, sums[:, :width], precision=HIGHEST, preferred_element_type=F32) * (1.0 / (NY * NC))
    p_basis = jnp.dot(inverse, p_total[...], precision=HIGHEST, preferred_element_type=F32)
    compressed = lax.dot_general(p_basis, q_next, TN, precision=HIGHEST, preferred_element_type=F32)
    q_out[...] = q_next
    compressed_out[...] = compressed
    error_out[...] = merged[...] - compressed


def finish(place, mine, other, p_total, merged):
    rank = p_total.shape[0]
    return pl.pallas_call(
        finish_kernel,
        out_shape=(
            jax.ShapeDtypeStruct(merged.shape, F32),
            jax.ShapeDtypeStruct(merged.shape, F32),
            jax.ShapeDtypeStruct((rank, merged.shape[1]), F32),
        ),
        in_specs=[pl.BlockSpec(memory_space=pltpu.SMEM)] + [pl.BlockSpec(memory_space=pltpu.VMEM)] * 4,
        compiler_params=pltpu.CompilerParams(vmem_limit_bytes=32 * 1024 * 1024),
        name="finish",
    )(place, mine, other, p_total, merged)


def local(activations, cotangent, kv_weight, error_buffer, q_start):
    c, x, z = (lax.axis_index(a) for a in "cxz")
    place = jnp.stack([x, c, z] + [x ^ k for k in PARTNERS]).astype(jnp.int32)
    error = error_buffer[0]

    with jax.named_scope("exchange"):
        sub = kv_weight.shape[0] // NC
        mine = lax.dynamic_slice_in_dim(kv_weight, c * sub, sub, axis=0)
        column = jnp.stack(swaps(mine, "x", NX))
        packed = pack(place, activations, cotangent)
        weight = lax.all_gather(column, "z", axis=0)
        pieces = [swap(packed[i], "x", NX, PARTNERS[i // 2]) for i in (0, 1, 4, 5, 2, 3)]

    with jax.named_scope("gradient"):
        part = gradient_terms(place, activations, cotangent, pieces)
        part, pieces = lax.optimization_barrier((part, pieces))
        gradient = lax.psum_scatter(part, "z", scatter_dimension=0, tiled=True)

    with jax.named_scope("left"):
        left = left_terms(place, q_start, error, activations, cotangent, pieces)
        left = tree(list(lax.all_to_all(left, ("y", "c"), 0, 0, tiled=True)))
        left = tree(list(lax.all_to_all(left, "z", 0, 0, tiled=True)))
        left = jnp.broadcast_to(left[None], (NY * NC,) + left.shape)
        p_total = lax.all_to_all(left, ("y", "c"), 0, 0, tiled=True).reshape(q_start.shape[0], -1)

    with jax.named_scope("weight"):
        input_grad = project(place, cotangent, weight, swap(weight, "c", NC, 1))

    with jax.named_scope("sums"):
        merged, keep, give = right_terms(place, input_grad[:16, :128], gradient, error, p_total)
        keep = keep + swap(give, "c", NC, 1)
        keep = tree(swaps(keep, "y", NY))
        keep = tree(swaps(keep, "x", NX))
        keep = keep + swap(keep, "z", NZ, 1)
        keep = tree([keep] + [swap(keep, "z", NZ, k) for k in (2, 4, 6)])
        other = swap(keep, "c", NC, 1)

    with jax.named_scope("finish"):
        error_next, compressed, q_next = finish(place, keep, other, p_total, merged)
    return (input_grad, error_next[None], compressed, q_next)


def solution(mesh):
    fine = Mesh(mesh.devices.reshape(NY, NC, NX, NZ), ("y", "c", "x", "z"))
    dp, fsdp = ("y", "c"), ("x", "z")
    return jax.shard_map(
        local,
        mesh=fine,
        in_specs=(P(dp + fsdp, None), P(dp + fsdp, None), P(fsdp, None), P(dp, fsdp, None), P()),
        out_specs=(P(dp + fsdp, None), P(dp, fsdp, None), P(fsdp, None), P()),
        check_vma=False,
    )
```

```python
import functools

import jax
import jax.numpy as jnp
from jax import lax
from jax.experimental import pallas as pl
from jax.experimental.pallas import tpu as pltpu
from jax.sharding import Mesh, PartitionSpec as P

LOSS_SCALE = 256.0
HIGHEST = lax.Precision.HIGHEST
F32 = jnp.float32
BF16 = jnp.bfloat16
NY, NC, NX, NZ = 4, 2, 4, 8
NT = (((1,), (1,)), ((), ()))
TN = (((0,), (0,)), ((), ()))


def swap(value, axis, size, k):
    return lax.ppermute(value, axis, [(i, i ^ k) for i in range(size)])


def swaps(value, axis, size):
    return [value] + [swap(value, axis, size, k) for k in range(1, size)]


def tree(parts):
    while len(parts) > 1:
        parts = [parts[i] + parts[i + 1] for i in range(0, len(parts), 2)]
    return parts[0]


def thirds(value):
    parts = []
    for _ in range(3):
        part = value.astype(BF16)
        parts.append(part)
        value = value - part.astype(F32)
    return jnp.concatenate(parts, axis=0)


def join(value):
    rank = value.shape[0] // 3
    return value[:rank] + (value[rank:2 * rank] + value[2 * rank:])


PARTNERS = (2, 1, 3)


def pack_kernel(place, act, cot, *refs):
    outs, arrived = refs[:-1], refs[-1]
    rows = outs[0].shape[0]
    columns = act.shape[1] // NX
    copies = []
    for i, out in enumerate(outs):
        here = pl.ds((i % 2) * rows, rows)
        start = pl.multiple_of(place[3 + i // 2] * columns, columns)
        copies.append((act.at[here, pl.ds(start, columns)], out.at[:, pl.ds(0, columns)]))
        copies.append((cot.at[here, :], out.at[:, pl.ds(columns, cot.shape[1])]))
    copies = [pltpu.make_async_copy(src, dst, arrived.at[i]) for i, (src, dst) in enumerate(copies)]
    for copy in copies:
        copy.start()
    for copy in copies:
        copy.wait()


def pack(place, activations, cotangent):
    tokens, width = cotangent.shape
    count = 2 * len(PARTNERS)
    shape = jax.ShapeDtypeStruct((tokens // 2, activations.shape[1] // NX + width), BF16)
    return pl.pallas_call(
        pack_kernel,
        out_shape=(shape,) * count,
        in_specs=[pl.BlockSpec(memory_space=pltpu.SMEM)] + [pl.BlockSpec(memory_space=pltpu.HBM)] * 2,
        out_specs=[pl.BlockSpec(memory_space=pltpu.VMEM)] * count,
        scratch_shapes=[pltpu.SemaphoreType.DMA((2 * count,))],
        cost_estimate=pl.CostEstimate(flops=0, bytes_accessed=2 * activations.size, transcendentals=0),
        compiler_params=pltpu.CompilerParams(vmem_limit_bytes=46 * 1024 * 1024),
        name="pack",
    )(place, activations, cotangent)


def load_tokens(refs, rows):
    at = 0
    for ref in refs:
        rows[at:at + ref.shape[0], :] = ref[...]
        at += ref.shape[0]


def gradient_kernel(count, place, *refs):
    cots, acts = refs[:count], refs[count:2 * count]
    gradient, lhs, cot_rows, rows = refs[2 * count:]

    @pl.when(pl.program_id(0) == 0)
    def _():
        load_tokens(cots, cot_rows)
        lhs[...] = cot_rows[...].T

    load_tokens(acts, rows)
    block = gradient.shape[2]
    for i in range(gradient.shape[0]):
        gradient[i] = jnp.dot(lhs[...], rows[:, i * block:(i + 1) * block], preferred_element_type=F32)


def left_kernel(count, place, q, error, *refs):
    cots, acts = refs[:count], refs[count:2 * count]
    left, lhs, cot_rows, rows = refs[2 * count:]
    z = pl.program_id(0)
    block = acts[0].shape[1]

    @pl.when(z == 0)
    def _():
        load_tokens(cots, cot_rows)
        q_cot = lax.dot_general(
            q[...], cot_rows[...].astype(F32), NT, precision=HIGHEST, preferred_element_type=F32
        )
        lhs[...] = thirds(q_cot)

    load_tokens(acts, rows)
    part = join(jnp.dot(lhs[...], rows[...], preferred_element_type=F32)) * (1.0 / LOSS_SCALE)
    left[:, 0] = part.reshape(NY * NC, -1, block)

    @pl.when(z == place[2])
    def _():
        own = lax.dot_general(q[...], error[...], NT, precision=HIGHEST, preferred_element_type=F32)
        left[:, 0] = left[:, 0] + own.reshape(NY * NC, -1, block)


def token_specs(activations, cotangent, pieces, steps):
    tokens, width = cotangent.shape
    block = activations.shape[1] // (NX * steps)
    part = pieces[0].shape[0]
    last = block * steps // width
    specs = [pl.BlockSpec((tokens, width), lambda i, place: (0, 0))]
    specs += [pl.BlockSpec((part, width), lambda i, place: (0, last))] * len(pieces)
    specs.append(pl.BlockSpec((tokens, block), lambda i, place: (0, place[0] * steps + i)))
    specs += [pl.BlockSpec((part, block), lambda i, place: (0, i))] * len(pieces)
    return specs


def gradient_terms(place, activations, cotangent, pieces):
    width = cotangent.shape[1]
    tokens = NX * cotangent.shape[0]
    columns = activations.shape[1] // NX
    steps = 4
    return pl.pallas_call(
        functools.partial(gradient_kernel, 1 + len(pieces)),
        out_shape=jax.ShapeDtypeStruct((NZ, width, columns // NZ), F32),
        grid_spec=pltpu.PrefetchScalarGridSpec(
            num_scalar_prefetch=1,
            grid=(steps,),
            in_specs=token_specs(activations, cotangent, pieces, steps),
            out_specs=pl.BlockSpec((NZ // steps, width, columns // NZ), lambda i, place: (i, 0, 0)),
            scratch_shapes=[
                pltpu.VMEM(shape, BF16) for shape in ((width, tokens), (tokens, width), (tokens, columns // steps))
            ],
        ),
        cost_estimate=pl.CostEstimate(
            flops=2 * width * tokens * columns,
            bytes_accessed=(2 * tokens + 4 * width) * columns,
            transcendentals=0,
        ),
        compiler_params=pltpu.CompilerParams(vmem_limit_bytes=52 * 1024 * 1024),
        name="gradient_terms",
    )(place, cotangent, *pieces, activations, *pieces)


def left_terms(place, q_start, error, activations, cotangent, pieces):
    rank, width = q_start.shape
    tokens = NX * cotangent.shape[0]
    block = activations.shape[1] // (NX * NZ)
    shares = NY * NC
    return pl.pallas_call(
        functools.partial(left_kernel, 1 + len(pieces)),
        out_shape=jax.ShapeDtypeStruct((shares, NZ, rank // shares, block), F32),
        grid_spec=pltpu.PrefetchScalarGridSpec(
            num_scalar_prefetch=1,
            grid=(NZ,),
            in_specs=[
                pl.BlockSpec((rank, width), lambda z, place: (0, 0)),
                pl.BlockSpec((block, width), lambda z, place: (0, 0)),
            ]
            + token_specs(activations, cotangent, pieces, NZ),
            out_specs=pl.BlockSpec((shares, 1, rank // shares, block), lambda z, place: (0, z, 0, 0)),
            scratch_shapes=[pltpu.VMEM(shape, BF16) for shape in ((3 * rank, tokens), (tokens, width), (tokens, block))],
        ),
        cost_estimate=pl.CostEstimate(
            flops=6 * rank * tokens * block * NZ,
            bytes_accessed=2 * tokens * block * NZ,
            transcendentals=0,
        ),
        compiler_params=pltpu.CompilerParams(vmem_limit_bytes=52 * 1024 * 1024),
        name="left_terms",
    )(place, q_start, error, cotangent, *pieces, activations, *pieces)


def project_kernel(place, cot, *rest):
    pieces, out, rows, arrived = rest[:NC * NX], rest[NC * NX], rest[NC * NX + 1], rest[NC * NX + 2]
    sub = pieces[0].shape[1]
    block = NC * sub

    def fetch(k, c):
        start = pl.multiple_of((place[1] ^ c) * sub, sub)
        return pltpu.make_async_copy(
            pieces[NC * k + c], rows.at[k, :, pl.ds(start, sub), :], arrived.at[NC * k + c]
        )

    @pl.when(pl.program_id(0) == 0)
    def _():
        for k in range(NX):
            for c in range(NC):
                fetch(k, c).start()

    for k in range(NX):
        @pl.when(pl.program_id(0) == k)
        def _():
            for c in range(NC):
                fetch(k, c).wait()
            for z in range(NZ):
                out[:, z * block:(z + 1) * block] = lax.dot_general(
                    cot[...], rows[k, z], NT, preferred_element_type=F32
                ).astype(BF16)


def project(place, cot, pieces):
    tokens, width = cot.shape
    sub = pieces[0].shape[1]
    columns = NZ * NC * sub
    return pl.pallas_call(
        project_kernel,
        out_shape=jax.ShapeDtypeStruct((tokens, NX * columns), BF16),
        grid_spec=pltpu.PrefetchScalarGridSpec(
            num_scalar_prefetch=1,
            grid=(NX,),
            in_specs=[pl.BlockSpec((tokens, width), lambda k, place: (0, 0))]
            + [pl.BlockSpec(memory_space=pltpu.HBM)] * (NC * NX),
            out_specs=pl.BlockSpec((tokens, columns), lambda k, place: (0, k ^ place[0])),
            scratch_shapes=[pltpu.VMEM((NX, NZ, NC * sub, width), BF16), pltpu.SemaphoreType.DMA((NC * NX,))],
        ),
        cost_estimate=pl.CostEstimate(
            flops=2 * tokens * width * NX * columns,
            bytes_accessed=2 * (tokens + width) * NX * columns,
            transcendentals=0,
        ),
        compiler_params=pltpu.CompilerParams(vmem_limit_bytes=62_000_000),
        name="project",
    )(place, cot, *pieces)


def right_kernel(place, _, gradient, error, p_total, merged_out, keep, give):
    half = keep.shape[0]
    merged = gradient[0].T * (1.0 / LOSS_SCALE) + error[...]
    merged_out[...] = merged
    p = p_total[...]
    right = jnp.dot(p, merged, precision=HIGHEST, preferred_element_type=F32)
    gram = lax.dot_general(p, p, NT, precision=HIGHEST, preferred_element_type=F32) * (1.0 / (NY * NC))
    sums = jnp.concatenate([right, gram], axis=1)
    first = place[1] == 0
    keep[...] = jnp.where(first, sums[:half], sums[half:])
    give[...] = jnp.where(first, sums[half:], sums[:half])


def right_terms(place, after, gradient, error, p_total):
    rank, width = p_total.shape[0], error.shape[1]
    half = jax.ShapeDtypeStruct((rank // NC, width + rank), F32)
    return pl.pallas_call(
        right_kernel,
        out_shape=(jax.ShapeDtypeStruct(error.shape, F32), half, half),
        in_specs=[pl.BlockSpec(memory_space=pltpu.SMEM), pl.BlockSpec(memory_space=pltpu.HBM)]
        + [pl.BlockSpec(memory_space=pltpu.VMEM)] * 3,
        compiler_params=pltpu.CompilerParams(vmem_limit_bytes=32 * 1024 * 1024),
        name="right_terms",
    )(place, after, gradient, error, p_total)


def eliminate(gram):
    rank = gram.shape[0]
    group = 4
    row = lax.broadcasted_iota(jnp.int32, (rank, 2 * rank), 0)
    col = lax.broadcasted_iota(jnp.int32, (rank, 2 * rank), 1)
    work = jnp.where(col == row + rank, 1.0, jnp.concatenate([gram, jnp.zeros_like(gram)], axis=1))
    scale = jnp.zeros_like(work)
    for base in range(0, rank, group):
        at = [base + j for j in range(group)]
        cols = [jnp.broadcast_to(work[:, k:k + 1], work.shape) for k in at]
        rows = [work[k:k + 1, :] for k in at]
        for j, k in enumerate(at):
            pivot = cols[j][k:k + 1, :]
            ratio = jnp.where(row > k, cols[j] * (1.0 / pivot), 0.0)
            scale = jnp.where(row == k, lax.rsqrt(pivot), scale)
            for i in range(j + 1, group):
                cols[i] = cols[i] - ratio * cols[i][k:k + 1, :]
                rows[i] = rows[i] - ratio[at[i]:at[i] + 1, :] * rows[j]
            work = work - ratio * rows[j]
    return (work * scale)[:, rank:]


def finish_kernel(place, mine, other, p_total, merged, error_out, compressed_out, q_out):
    width = merged.shape[1]
    first = place[1] == 0
    sums = jnp.concatenate([jnp.where(first, mine[...], other[...]), jnp.where(first, other[...], mine[...])], axis=0)
    inverse = eliminate(sums[:, width:])
    q_next = jnp.dot(inverse, sums[:, :width], precision=HIGHEST, preferred_element_type=F32) * (1.0 / (NY * NC))
    p_basis = jnp.dot(inverse, p_total[...], precision=HIGHEST, preferred_element_type=F32)
    compressed = lax.dot_general(p_basis, q_next, TN, precision=HIGHEST, preferred_element_type=F32)
    q_out[...] = q_next
    compressed_out[...] = compressed
    error_out[...] = merged[...] - compressed


def finish(place, mine, other, p_total, merged):
    rank = p_total.shape[0]
    return pl.pallas_call(
        finish_kernel,
        out_shape=(
            jax.ShapeDtypeStruct(merged.shape, F32),
            jax.ShapeDtypeStruct(merged.shape, F32),
            jax.ShapeDtypeStruct((rank, merged.shape[1]), F32),
        ),
        in_specs=[pl.BlockSpec(memory_space=pltpu.SMEM)] + [pl.BlockSpec(memory_space=pltpu.VMEM)] * 4,
        compiler_params=pltpu.CompilerParams(vmem_limit_bytes=32 * 1024 * 1024),
        name="finish",
    )(place, mine, other, p_total, merged)


def local(activations, cotangent, kv_weight, error_buffer, q_start):
    c, x, z = (lax.axis_index(a) for a in "cxz")
    place = jnp.stack([x, c, z] + [x ^ k for k in PARTNERS]).astype(jnp.int32)
    error = error_buffer[0]

    with jax.named_scope("exchange"):
        sub = kv_weight.shape[0] // NC
        line = lax.all_gather(kv_weight, "z", axis=0)
        packed = pack(place, activations, cotangent)
        pieces = [swap(packed[i], "x", NX, PARTNERS[i // 2]) for i in (0, 1, 4, 5, 2, 3)]

    with jax.named_scope("gradient"):
        part = gradient_terms(place, activations, cotangent, pieces)
        part, pieces, line = lax.optimization_barrier((part, pieces, line))
        gradient = lax.psum_scatter(part, "z", scatter_dimension=0, tiled=True)

    with jax.named_scope("weight"):
        halves = swaps(lax.dynamic_slice_in_dim(line, c * sub, sub, axis=1), "x", NX)

    with jax.named_scope("left"):
        left = left_terms(place, q_start, error, activations, cotangent, pieces)
        left = tree(list(lax.all_to_all(left, ("y", "c"), 0, 0, tiled=True)))
        left = tree(list(lax.all_to_all(left, "z", 0, 0, tiled=True)))
        left, halves = lax.optimization_barrier((left, halves))
        left = jnp.broadcast_to(left[None], (NY * NC,) + left.shape)
        p_total = lax.all_to_all(left, ("y", "c"), 0, 0, tiled=True).reshape(q_start.shape[0], -1)

    with jax.named_scope("weight"):
        weights = []
        for half in halves:
            weights += [half, swap(half, "c", NC, 1)]
        input_grad = project(place, cotangent, weights)

    with jax.named_scope("sums"):
        merged, keep, give = right_terms(place, input_grad[:16, :128], gradient, error, p_total)
        keep = keep + swap(give, "c", NC, 1)
        keep = tree(swaps(keep, "y", NY))
        keep = tree(swaps(keep, "x", NX))
        keep = keep + swap(keep, "z", NZ, 1)
        keep = tree([keep] + [swap(keep, "z", NZ, k) for k in (2, 4, 6)])
        other = swap(keep, "c", NC, 1)

    with jax.named_scope("finish"):
        error_next, compressed, q_next = finish(place, keep, other, p_total, merged)
    return (input_grad, error_next[None], compressed, q_next)


def solution(mesh):
    fine = Mesh(mesh.devices.reshape(NY, NC, NX, NZ), ("y", "c", "x", "z"))
    dp, fsdp = ("y", "c"), ("x", "z")
    return jax.shard_map(
        local,
        mesh=fine,
        in_specs=(P(dp + fsdp, None), P(dp + fsdp, None), P(fsdp, None), P(dp, fsdp, None), P()),
        out_specs=(P(dp + fsdp, None), P(dp, fsdp, None), P(fsdp, None), P()),
        check_vma=False,
    )
```

```python
import functools

import jax
import jax.numpy as jnp
from jax import lax
from jax.experimental import pallas as pl
from jax.experimental.pallas import tpu as pltpu
from jax.sharding import Mesh, PartitionSpec as P

LOSS_SCALE = 256.0
HIGHEST = lax.Precision.HIGHEST
F32 = jnp.float32
BF16 = jnp.bfloat16
NY, NC, NX, NZ = 4, 2, 4, 8
NT = (((1,), (1,)), ((), ()))
TN = (((0,), (0,)), ((), ()))


def swap(value, axis, size, k):
    return lax.ppermute(value, axis, [(i, i ^ k) for i in range(size)])


def swaps(value, axis, size):
    return [value] + [swap(value, axis, size, k) for k in range(1, size)]


def tree(parts):
    while len(parts) > 1:
        parts = [parts[i] + parts[i + 1] for i in range(0, len(parts), 2)]
    return parts[0]


def thirds(value):
    parts = []
    for _ in range(3):
        part = value.astype(BF16)
        parts.append(part)
        value = value - part.astype(F32)
    return jnp.concatenate(parts, axis=0)


def join(value):
    rank = value.shape[0] // 3
    return value[:rank] + (value[rank:2 * rank] + value[2 * rank:])


PARTNERS = (2, 1, 3)


def pack_kernel(place, act, cot, *refs):
    outs, arrived = refs[:-1], refs[-1]
    rows = outs[0].shape[0]
    columns = act.shape[1] // NX
    copies = []
    for i, out in enumerate(outs):
        here = pl.ds((i % 2) * rows, rows)
        start = pl.multiple_of(place[3 + i // 2] * columns, columns)
        copies.append((act.at[here, pl.ds(start, columns)], out.at[:, pl.ds(0, columns)]))
        copies.append((cot.at[here, :], out.at[:, pl.ds(columns, cot.shape[1])]))
    copies = [pltpu.make_async_copy(src, dst, arrived.at[i]) for i, (src, dst) in enumerate(copies)]
    for copy in copies:
        copy.start()
    for copy in copies:
        copy.wait()


def pack(place, activations, cotangent):
    tokens, width = cotangent.shape
    count = 2 * len(PARTNERS)
    shape = jax.ShapeDtypeStruct((tokens // 2, activations.shape[1] // NX + width), BF16)
    return pl.pallas_call(
        pack_kernel,
        out_shape=(shape,) * count,
        in_specs=[pl.BlockSpec(memory_space=pltpu.SMEM)] + [pl.BlockSpec(memory_space=pltpu.HBM)] * 2,
        out_specs=[pl.BlockSpec(memory_space=pltpu.VMEM)] * count,
        scratch_shapes=[pltpu.SemaphoreType.DMA((2 * count,))],
        cost_estimate=pl.CostEstimate(flops=0, bytes_accessed=2 * activations.size, transcendentals=0),
        compiler_params=pltpu.CompilerParams(vmem_limit_bytes=46 * 1024 * 1024),
        name="pack",
    )(place, activations, cotangent)


def load_tokens(refs, rows):
    at = 0
    for ref in refs:
        rows[at:at + ref.shape[0], :] = ref[...]
        at += ref.shape[0]


def gradient_kernel(count, place, *refs):
    cots, acts = refs[:count], refs[count:2 * count]
    gradient, lhs, cot_rows, rows = refs[2 * count:]

    @pl.when(pl.program_id(0) == 0)
    def _():
        load_tokens(cots, cot_rows)
        lhs[...] = cot_rows[...].T

    load_tokens(acts, rows)
    block = gradient.shape[2]
    for i in range(gradient.shape[0]):
        gradient[i] = jnp.dot(lhs[...], rows[:, i * block:(i + 1) * block], preferred_element_type=F32)


def left_kernel(count, place, q, error, *refs):
    cots, acts = refs[:count], refs[count:2 * count]
    left, lhs, cot_rows, rows = refs[2 * count:]
    z = pl.program_id(0)
    block = acts[0].shape[1]

    @pl.when(z == 0)
    def _():
        load_tokens(cots, cot_rows)
        q_cot = lax.dot_general(
            q[...], cot_rows[...].astype(F32), NT, precision=HIGHEST, preferred_element_type=F32
        )
        lhs[...] = thirds(q_cot)

    load_tokens(acts, rows)
    part = join(jnp.dot(lhs[...], rows[...], preferred_element_type=F32)) * (1.0 / LOSS_SCALE)
    left[:, 0] = part.reshape(NY * NC, -1, block)

    @pl.when(z == place[2])
    def _():
        own = lax.dot_general(q[...], error[...], NT, precision=HIGHEST, preferred_element_type=F32)
        left[:, 0] = left[:, 0] + own.reshape(NY * NC, -1, block)


def token_specs(activations, cotangent, pieces, steps):
    tokens, width = cotangent.shape
    block = activations.shape[1] // (NX * steps)
    part = pieces[0].shape[0]
    last = block * steps // width
    specs = [pl.BlockSpec((tokens, width), lambda i, place: (0, 0))]
    specs += [pl.BlockSpec((part, width), lambda i, place: (0, last))] * len(pieces)
    specs.append(pl.BlockSpec((tokens, block), lambda i, place: (0, place[0] * steps + i)))
    specs += [pl.BlockSpec((part, block), lambda i, place: (0, i))] * len(pieces)
    return specs


def gradient_terms(place, activations, cotangent, pieces):
    width = cotangent.shape[1]
    tokens = NX * cotangent.shape[0]
    columns = activations.shape[1] // NX
    steps = 4
    return pl.pallas_call(
        functools.partial(gradient_kernel, 1 + len(pieces)),
        out_shape=jax.ShapeDtypeStruct((NZ, width, columns // NZ), F32),
        grid_spec=pltpu.PrefetchScalarGridSpec(
            num_scalar_prefetch=1,
            grid=(steps,),
            in_specs=token_specs(activations, cotangent, pieces, steps),
            out_specs=pl.BlockSpec((NZ // steps, width, columns // NZ), lambda i, place: (i, 0, 0)),
            scratch_shapes=[
                pltpu.VMEM(shape, BF16) for shape in ((width, tokens), (tokens, width), (tokens, columns // steps))
            ],
        ),
        cost_estimate=pl.CostEstimate(
            flops=2 * width * tokens * columns,
            bytes_accessed=(2 * tokens + 4 * width) * columns,
            transcendentals=0,
        ),
        compiler_params=pltpu.CompilerParams(vmem_limit_bytes=52 * 1024 * 1024),
        name="gradient_terms",
    )(place, cotangent, *pieces, activations, *pieces)


def left_terms(place, q_start, error, activations, cotangent, pieces):
    rank, width = q_start.shape
    tokens = NX * cotangent.shape[0]
    block = activations.shape[1] // (NX * NZ)
    shares = NY * NC
    return pl.pallas_call(
        functools.partial(left_kernel, 1 + len(pieces)),
        out_shape=jax.ShapeDtypeStruct((shares, NZ, rank // shares, block), F32),
        grid_spec=pltpu.PrefetchScalarGridSpec(
            num_scalar_prefetch=1,
            grid=(NZ,),
            in_specs=[
                pl.BlockSpec((rank, width), lambda z, place: (0, 0)),
                pl.BlockSpec((block, width), lambda z, place: (0, 0)),
            ]
            + token_specs(activations, cotangent, pieces, NZ),
            out_specs=pl.BlockSpec((shares, 1, rank // shares, block), lambda z, place: (0, z, 0, 0)),
            scratch_shapes=[pltpu.VMEM(shape, BF16) for shape in ((3 * rank, tokens), (tokens, width), (tokens, block))],
        ),
        cost_estimate=pl.CostEstimate(
            flops=6 * rank * tokens * block * NZ,
            bytes_accessed=2 * tokens * block * NZ,
            transcendentals=0,
        ),
        compiler_params=pltpu.CompilerParams(vmem_limit_bytes=52 * 1024 * 1024),
        name="left_terms",
    )(place, q_start, error, cotangent, *pieces, activations, *pieces)


def project_kernel(place, cot, *rest):
    pieces, out, rows, arrived = rest[:NC * NX], rest[NC * NX], rest[NC * NX + 1], rest[NC * NX + 2]
    sub = pieces[0].shape[1]
    block = NC * sub

    def fetch(k, c):
        start = pl.multiple_of((place[1] ^ c) * sub, sub)
        return pltpu.make_async_copy(
            pieces[NC * k + c], rows.at[k, :, pl.ds(start, sub), :], arrived.at[NC * k + c]
        )

    @pl.when(pl.program_id(0) == 0)
    def _():
        for k in range(NX):
            for c in range(NC):
                fetch(k, c).start()

    for k in range(NX):
        @pl.when(pl.program_id(0) == k)
        def _():
            for c in range(NC):
                fetch(k, c).wait()
            for z in range(NZ):
                out[:, z * block:(z + 1) * block] = lax.dot_general(
                    cot[...], rows[k, z], NT, preferred_element_type=F32
                ).astype(BF16)


def project(place, cot, pieces):
    tokens, width = cot.shape
    sub = pieces[0].shape[1]
    columns = NZ * NC * sub
    return pl.pallas_call(
        project_kernel,
        out_shape=jax.ShapeDtypeStruct((tokens, NX * columns), BF16),
        grid_spec=pltpu.PrefetchScalarGridSpec(
            num_scalar_prefetch=1,
            grid=(NX,),
            in_specs=[pl.BlockSpec((tokens, width), lambda k, place: (0, 0))]
            + [pl.BlockSpec(memory_space=pltpu.HBM)] * (NC * NX),
            out_specs=pl.BlockSpec((tokens, columns), lambda k, place: (0, k ^ place[0])),
            scratch_shapes=[pltpu.VMEM((NX, NZ, NC * sub, width), BF16), pltpu.SemaphoreType.DMA((NC * NX,))],
        ),
        cost_estimate=pl.CostEstimate(
            flops=2 * tokens * width * NX * columns,
            bytes_accessed=2 * (tokens + width) * NX * columns,
            transcendentals=0,
        ),
        compiler_params=pltpu.CompilerParams(vmem_limit_bytes=62_000_000),
        name="project",
    )(place, cot, *pieces)


def right_kernel(place, _, gradient, error, p_total, merged_out, keep, give):
    half = keep.shape[0]
    merged = gradient[0].T * (1.0 / LOSS_SCALE) + error[...]
    merged_out[...] = merged
    p = p_total[...]
    right = jnp.dot(p, merged, precision=HIGHEST, preferred_element_type=F32)
    gram = lax.dot_general(p, p, NT, precision=HIGHEST, preferred_element_type=F32) * (1.0 / (NY * NC))
    sums = jnp.concatenate([right, gram], axis=1)
    first = place[1] == 0
    keep[...] = jnp.where(first, sums[:half], sums[half:])
    give[...] = jnp.where(first, sums[half:], sums[:half])


def right_terms(place, after, gradient, error, p_total):
    rank, width = p_total.shape[0], error.shape[1]
    half = jax.ShapeDtypeStruct((rank // NC, width + rank), F32)
    return pl.pallas_call(
        right_kernel,
        out_shape=(jax.ShapeDtypeStruct(error.shape, F32), half, half),
        in_specs=[pl.BlockSpec(memory_space=pltpu.SMEM), pl.BlockSpec(memory_space=pltpu.HBM)]
        + [pl.BlockSpec(memory_space=pltpu.VMEM)] * 3,
        compiler_params=pltpu.CompilerParams(vmem_limit_bytes=32 * 1024 * 1024),
        name="right_terms",
    )(place, after, gradient, error, p_total)


def add_kernel(_, *refs):
    refs[-1][...] = tree([ref[...] for ref in refs[:-1]])


def add_after(after, parts):
    return pl.pallas_call(
        add_kernel,
        out_shape=jax.ShapeDtypeStruct(parts[0].shape, F32),
        compiler_params=pltpu.CompilerParams(vmem_limit_bytes=4 * 1024 * 1024),
        name="add_after",
    )(after, *parts)


def eliminate(gram):
    rank = gram.shape[0]
    group = 4
    row = lax.broadcasted_iota(jnp.int32, (rank, 2 * rank), 0)
    col = lax.broadcasted_iota(jnp.int32, (rank, 2 * rank), 1)
    work = jnp.where(col == row + rank, 1.0, jnp.concatenate([gram, jnp.zeros_like(gram)], axis=1))
    scale = jnp.zeros_like(work)
    for base in range(0, rank, group):
        at = [base + j for j in range(group)]
        cols = [jnp.broadcast_to(work[:, k:k + 1], work.shape) for k in at]
        rows = [work[k:k + 1, :] for k in at]
        for j, k in enumerate(at):
            pivot = cols[j][k:k + 1, :]
            ratio = jnp.where(row > k, cols[j] * (1.0 / pivot), 0.0)
            scale = jnp.where(row == k, lax.rsqrt(pivot), scale)
            for i in range(j + 1, group):
                cols[i] = cols[i] - ratio * cols[i][k:k + 1, :]
                rows[i] = rows[i] - ratio[at[i]:at[i] + 1, :] * rows[j]
            work = work - ratio * rows[j]
    return (work * scale)[:, rank:]


def finish_kernel(place, mine, other, p_total, merged, error_out, compressed_out, q_out):
    width = merged.shape[1]
    first = place[1] == 0
    sums = jnp.concatenate([jnp.where(first, mine[...], other[...]), jnp.where(first, other[...], mine[...])], axis=0)
    inverse = eliminate(sums[:, width:])
    q_next = jnp.dot(inverse, sums[:, :width], precision=HIGHEST, preferred_element_type=F32) * (1.0 / (NY * NC))
    p_basis = jnp.dot(inverse, p_total[...], precision=HIGHEST, preferred_element_type=F32)
    compressed = lax.dot_general(p_basis, q_next, TN, precision=HIGHEST, preferred_element_type=F32)
    q_out[...] = q_next
    compressed_out[...] = compressed
    error_out[...] = merged[...] - compressed


def finish(place, mine, other, p_total, merged):
    rank = p_total.shape[0]
    return pl.pallas_call(
        finish_kernel,
        out_shape=(
            jax.ShapeDtypeStruct(merged.shape, F32),
            jax.ShapeDtypeStruct(merged.shape, F32),
            jax.ShapeDtypeStruct((rank, merged.shape[1]), F32),
        ),
        in_specs=[pl.BlockSpec(memory_space=pltpu.SMEM)] + [pl.BlockSpec(memory_space=pltpu.VMEM)] * 4,
        compiler_params=pltpu.CompilerParams(vmem_limit_bytes=32 * 1024 * 1024),
        name="finish",
    )(place, mine, other, p_total, merged)


def local(activations, cotangent, kv_weight, error_buffer, q_start):
    c, x, z = (lax.axis_index(a) for a in "cxz")
    place = jnp.stack([x, c, z] + [x ^ k for k in PARTNERS]).astype(jnp.int32)
    error = error_buffer[0]

    with jax.named_scope("exchange"):
        sub = kv_weight.shape[0] // NC
        line = lax.all_gather(kv_weight, "z", axis=0)
        packed = pack(place, activations, cotangent)
        pieces = [swap(packed[i], "x", NX, PARTNERS[i // 2]) for i in (0, 1, 4, 5, 2, 3)]

    with jax.named_scope("gradient"):
        part = gradient_terms(place, activations, cotangent, pieces)
        part, pieces, line = lax.optimization_barrier((part, pieces, line))
        gradient = lax.psum_scatter(part, "z", scatter_dimension=0, tiled=True)

    with jax.named_scope("weight"):
        halves = swaps(lax.dynamic_slice_in_dim(line, c * sub, sub, axis=1), "x", NX)

    with jax.named_scope("left"):
        left = left_terms(place, q_start, error, activations, cotangent, pieces)
        left = tree(list(lax.all_to_all(left, ("y", "c"), 0, 0, tiled=True)))
        left = tree(list(lax.all_to_all(left, "z", 0, 0, tiled=True)))
        left, halves = lax.optimization_barrier((left, halves))
        left = jnp.broadcast_to(left[None], (NY * NC,) + left.shape)
        p_total = lax.all_to_all(left, ("y", "c"), 0, 0, tiled=True).reshape(q_start.shape[0], -1)

    with jax.named_scope("weight"):
        weights = []
        for half in halves:
            weights += [half, swap(half, "c", NC, 1)]
        input_grad = project(place, cotangent, weights)
        swapped = tree([half[0, :16, :128] for half in weights[1::2]])

    with jax.named_scope("sums"):
        merged, keep, give = right_terms(place, swapped, gradient, error, p_total)
        keep = keep + swap(give, "c", NC, 1)
        keep = tree(swaps(keep, "y", NY))
        keep = add_after(input_grad[:16, :128], swaps(keep, "x", NX))
        keep = keep + swap(keep, "z", NZ, 1)
        keep = tree([keep] + [swap(keep, "z", NZ, k) for k in (2, 4, 6)])
        other = swap(keep, "c", NC, 1)

    with jax.named_scope("finish"):
        error_next, compressed, q_next = finish(place, keep, other, p_total, merged)
    return (input_grad, error_next[None], compressed, q_next)


def solution(mesh):
    fine = Mesh(mesh.devices.reshape(NY, NC, NX, NZ), ("y", "c", "x", "z"))
    dp, fsdp = ("y", "c"), ("x", "z")
    return jax.shard_map(
        local,
        mesh=fine,
        in_specs=(P(dp + fsdp, None), P(dp + fsdp, None), P(fsdp, None), P(dp, fsdp, None), P()),
        out_specs=(P(dp + fsdp, None), P(dp, fsdp, None), P(fsdp, None), P()),
        check_vma=False,
    )
```

```python
import functools

import jax
import jax.numpy as jnp
from jax import lax
from jax.experimental import pallas as pl
from jax.experimental.pallas import tpu as pltpu
from jax.sharding import Mesh, PartitionSpec as P

LOSS_SCALE = 256.0
HIGHEST = lax.Precision.HIGHEST
F32 = jnp.float32
BF16 = jnp.bfloat16
NY, NC, NX, NZ = 4, 2, 4, 8
NT = (((1,), (1,)), ((), ()))
TN = (((0,), (0,)), ((), ()))


def swap(value, axis, size, k):
    return lax.ppermute(value, axis, [(i, i ^ k) for i in range(size)])


def swaps(value, axis, size):
    return [value] + [swap(value, axis, size, k) for k in range(1, size)]


def tree(parts):
    while len(parts) > 1:
        parts = [parts[i] + parts[i + 1] for i in range(0, len(parts), 2)]
    return parts[0]


def thirds(value):
    parts = []
    for _ in range(3):
        part = value.astype(BF16)
        parts.append(part)
        value = value - part.astype(F32)
    return jnp.concatenate(parts, axis=0)


def join(value):
    rank = value.shape[0] // 3
    return value[:rank] + (value[rank:2 * rank] + value[2 * rank:])


PARTNERS = (2, 1, 3)


def pack_kernel(place, act, cot, *refs):
    outs, arrived = refs[:-1], refs[-1]
    rows = outs[0].shape[0]
    columns = act.shape[1] // NX
    copies = []
    for i, out in enumerate(outs):
        here = pl.ds((i % 2) * rows, rows)
        start = pl.multiple_of(place[3 + i // 2] * columns, columns)
        copies.append((act.at[here, pl.ds(start, columns)], out.at[:, pl.ds(0, columns)]))
        copies.append((cot.at[here, :], out.at[:, pl.ds(columns, cot.shape[1])]))
    copies = [pltpu.make_async_copy(src, dst, arrived.at[i]) for i, (src, dst) in enumerate(copies)]
    for copy in copies:
        copy.start()
    for copy in copies:
        copy.wait()


def pack(place, activations, cotangent):
    tokens, width = cotangent.shape
    count = 2 * len(PARTNERS)
    shape = jax.ShapeDtypeStruct((tokens // 2, activations.shape[1] // NX + width), BF16)
    return pl.pallas_call(
        pack_kernel,
        out_shape=(shape,) * count,
        in_specs=[pl.BlockSpec(memory_space=pltpu.SMEM)] + [pl.BlockSpec(memory_space=pltpu.HBM)] * 2,
        out_specs=[pl.BlockSpec(memory_space=pltpu.VMEM)] * count,
        scratch_shapes=[pltpu.SemaphoreType.DMA((2 * count,))],
        cost_estimate=pl.CostEstimate(flops=0, bytes_accessed=2 * activations.size, transcendentals=0),
        compiler_params=pltpu.CompilerParams(vmem_limit_bytes=46 * 1024 * 1024),
        name="pack",
    )(place, activations, cotangent)


def load_tokens(refs, rows):
    at = 0
    for ref in refs:
        rows[at:at + ref.shape[0], :] = ref[...]
        at += ref.shape[0]


def gradient_kernel(count, place, *refs):
    cots, acts = refs[:count], refs[count:2 * count]
    gradient, lhs, cot_rows, rows = refs[2 * count:]

    @pl.when(pl.program_id(0) == 0)
    def _():
        load_tokens(cots, cot_rows)
        lhs[...] = cot_rows[...].T

    load_tokens(acts, rows)
    block = gradient.shape[2]
    for i in range(gradient.shape[0]):
        gradient[i] = jnp.dot(lhs[...], rows[:, i * block:(i + 1) * block], preferred_element_type=F32)


def left_kernel(count, place, q, error, *refs):
    cots, acts = refs[:count], refs[count:2 * count]
    left, lhs, cot_rows, rows = refs[2 * count:]
    z = pl.program_id(0)
    block = acts[0].shape[1]

    @pl.when(z == 0)
    def _():
        load_tokens(cots, cot_rows)
        q_cot = lax.dot_general(
            q[...], cot_rows[...].astype(F32), NT, precision=HIGHEST, preferred_element_type=F32
        )
        lhs[...] = thirds(q_cot)

    load_tokens(acts, rows)
    part = join(jnp.dot(lhs[...], rows[...], preferred_element_type=F32)) * (1.0 / LOSS_SCALE)
    left[:, 0] = part.reshape(NY * NC, -1, block)

    @pl.when(z == place[2])
    def _():
        own = lax.dot_general(q[...], error[...], NT, precision=HIGHEST, preferred_element_type=F32)
        left[:, 0] = left[:, 0] + own.reshape(NY * NC, -1, block)


def token_specs(activations, cotangent, pieces, steps):
    tokens, width = cotangent.shape
    block = activations.shape[1] // (NX * steps)
    part = pieces[0].shape[0]
    last = block * steps // width
    specs = [pl.BlockSpec((tokens, width), lambda i, place: (0, 0))]
    specs += [pl.BlockSpec((part, width), lambda i, place: (0, last))] * len(pieces)
    specs.append(pl.BlockSpec((tokens, block), lambda i, place: (0, place[0] * steps + i)))
    specs += [pl.BlockSpec((part, block), lambda i, place: (0, i))] * len(pieces)
    return specs


def gradient_terms(place, activations, cotangent, pieces):
    width = cotangent.shape[1]
    tokens = NX * cotangent.shape[0]
    columns = activations.shape[1] // NX
    steps = 4
    return pl.pallas_call(
        functools.partial(gradient_kernel, 1 + len(pieces)),
        out_shape=jax.ShapeDtypeStruct((NZ, width, columns // NZ), F32),
        grid_spec=pltpu.PrefetchScalarGridSpec(
            num_scalar_prefetch=1,
            grid=(steps,),
            in_specs=token_specs(activations, cotangent, pieces, steps),
            out_specs=pl.BlockSpec((NZ // steps, width, columns // NZ), lambda i, place: (i, 0, 0)),
            scratch_shapes=[
                pltpu.VMEM(shape, BF16) for shape in ((width, tokens), (tokens, width), (tokens, columns // steps))
            ],
        ),
        cost_estimate=pl.CostEstimate(
            flops=2 * width * tokens * columns,
            bytes_accessed=(2 * tokens + 4 * width) * columns,
            transcendentals=0,
        ),
        compiler_params=pltpu.CompilerParams(vmem_limit_bytes=52 * 1024 * 1024),
        name="gradient_terms",
    )(place, cotangent, *pieces, activations, *pieces)


def left_terms(place, q_start, error, activations, cotangent, pieces):
    rank, width = q_start.shape
    tokens = NX * cotangent.shape[0]
    block = activations.shape[1] // (NX * NZ)
    shares = NY * NC
    return pl.pallas_call(
        functools.partial(left_kernel, 1 + len(pieces)),
        out_shape=jax.ShapeDtypeStruct((shares, NZ, rank // shares, block), F32),
        grid_spec=pltpu.PrefetchScalarGridSpec(
            num_scalar_prefetch=1,
            grid=(NZ,),
            in_specs=[
                pl.BlockSpec((rank, width), lambda z, place: (0, 0)),
                pl.BlockSpec((block, width), lambda z, place: (0, 0)),
            ]
            + token_specs(activations, cotangent, pieces, NZ),
            out_specs=pl.BlockSpec((shares, 1, rank // shares, block), lambda z, place: (0, z, 0, 0)),
            scratch_shapes=[pltpu.VMEM(shape, BF16) for shape in ((3 * rank, tokens), (tokens, width), (tokens, block))],
        ),
        cost_estimate=pl.CostEstimate(
            flops=6 * rank * tokens * block * NZ,
            bytes_accessed=2 * tokens * block * NZ,
            transcendentals=0,
        ),
        compiler_params=pltpu.CompilerParams(vmem_limit_bytes=52 * 1024 * 1024),
        name="left_terms",
    )(place, q_start, error, cotangent, *pieces, activations, *pieces)


def project_kernel(first, place, cot, *rest):
    count = NX // 2
    pieces, refs = rest[:NC * count], rest[NC * count:]
    out, flag, rows, arrived = refs[-4:]
    sub = pieces[0].shape[1]
    block = NC * sub

    def fetch(k, c):
        start = pl.multiple_of((place[1] ^ c) * sub, sub)
        return pltpu.make_async_copy(
            pieces[NC * k + c], rows.at[k, :, pl.ds(start, sub), :], arrived.at[NC * k + c]
        )

    @pl.when(pl.program_id(0) == 0)
    def _():
        flag[...] = jnp.zeros_like(flag)
        for k in range(count):
            for c in range(NC):
                fetch(k, c).start()

    for k in range(count):
        @pl.when(pl.program_id(0) == k)
        def _():
            for c in range(NC):
                fetch(k, c).wait()
            for z in range(NZ):
                out[:, z * block:(z + 1) * block] = lax.dot_general(
                    cot[...], rows[k, z], NT, preferred_element_type=F32
                ).astype(BF16)


def project(place, cot, pieces, first, earlier):
    tokens, width = cot.shape
    sub = pieces[0].shape[1]
    count = NX // 2
    columns = NZ * NC * sub
    return pl.pallas_call(
        functools.partial(project_kernel, first),
        out_shape=(jax.ShapeDtypeStruct((tokens, NX * columns), BF16), jax.ShapeDtypeStruct((8, 128), F32)),
        grid_spec=pltpu.PrefetchScalarGridSpec(
            num_scalar_prefetch=1,
            grid=(count,),
            in_specs=[pl.BlockSpec((tokens, width), lambda k, place: (0, 0))]
            + [pl.BlockSpec(memory_space=pltpu.HBM)] * (NC * count + len(earlier)),
            out_specs=(
                pl.BlockSpec((tokens, columns), lambda k, place: (0, (first + k) ^ place[0])),
                pl.BlockSpec((8, 128), lambda k, place: (0, 0)),
            ),
            scratch_shapes=[
                pltpu.VMEM((count, NZ, NC * sub, width), BF16),
                pltpu.SemaphoreType.DMA((NC * count,)),
            ],
        ),
        input_output_aliases={2 + NC * count: 0} if earlier else {},
        cost_estimate=pl.CostEstimate(
            flops=2 * tokens * width * count * columns,
            bytes_accessed=2 * (tokens + width) * count * columns,
            transcendentals=0,
        ),
        compiler_params=pltpu.CompilerParams(vmem_limit_bytes=62_000_000),
        name="project",
    )(place, cot, *pieces, *earlier)


def right_kernel(place, _, gradient, error, p_total, merged_out, keep, give):
    half = keep.shape[0]
    merged = gradient[0].T * (1.0 / LOSS_SCALE) + error[...]
    merged_out[...] = merged
    p = p_total[...]
    right = jnp.dot(p, merged, precision=HIGHEST, preferred_element_type=F32)
    gram = lax.dot_general(p, p, NT, precision=HIGHEST, preferred_element_type=F32) * (1.0 / (NY * NC))
    sums = jnp.concatenate([right, gram], axis=1)
    first = place[1] == 0
    keep[...] = jnp.where(first, sums[:half], sums[half:])
    give[...] = jnp.where(first, sums[half:], sums[:half])


def right_terms(place, after, gradient, error, p_total):
    rank, width = p_total.shape[0], error.shape[1]
    half = jax.ShapeDtypeStruct((rank // NC, width + rank), F32)
    return pl.pallas_call(
        right_kernel,
        out_shape=(jax.ShapeDtypeStruct(error.shape, F32), half, half),
        in_specs=[pl.BlockSpec(memory_space=pltpu.SMEM), pl.BlockSpec(memory_space=pltpu.HBM)]
        + [pl.BlockSpec(memory_space=pltpu.VMEM)] * 3,
        compiler_params=pltpu.CompilerParams(vmem_limit_bytes=32 * 1024 * 1024),
        name="right_terms",
    )(place, after, gradient, error, p_total)


def add_kernel(_, *refs):
    refs[-1][...] = tree([ref[...] for ref in refs[:-1]])


def add_after(after, parts):
    return pl.pallas_call(
        add_kernel,
        out_shape=jax.ShapeDtypeStruct(parts[0].shape, F32),
        compiler_params=pltpu.CompilerParams(vmem_limit_bytes=4 * 1024 * 1024),
        name="add_after",
    )(after, *parts)


def eliminate(gram):
    rank = gram.shape[0]
    group = 4
    row = lax.broadcasted_iota(jnp.int32, (rank, 2 * rank), 0)
    col = lax.broadcasted_iota(jnp.int32, (rank, 2 * rank), 1)
    work = jnp.where(col == row + rank, 1.0, jnp.concatenate([gram, jnp.zeros_like(gram)], axis=1))
    scale = jnp.zeros_like(work)
    for base in range(0, rank, group):
        at = [base + j for j in range(group)]
        cols = [jnp.broadcast_to(work[:, k:k + 1], work.shape) for k in at]
        rows = [work[k:k + 1, :] for k in at]
        for j, k in enumerate(at):
            pivot = cols[j][k:k + 1, :]
            ratio = jnp.where(row > k, cols[j] * (1.0 / pivot), 0.0)
            scale = jnp.where(row == k, lax.rsqrt(pivot), scale)
            for i in range(j + 1, group):
                cols[i] = cols[i] - ratio * cols[i][k:k + 1, :]
                rows[i] = rows[i] - ratio[at[i]:at[i] + 1, :] * rows[j]
            work = work - ratio * rows[j]
    return (work * scale)[:, rank:]


def finish_kernel(place, mine, other, p_total, merged, error_out, compressed_out, q_out):
    width = merged.shape[1]
    first = place[1] == 0
    sums = jnp.concatenate([jnp.where(first, mine[...], other[...]), jnp.where(first, other[...], mine[...])], axis=0)
    inverse = eliminate(sums[:, width:])
    q_next = jnp.dot(inverse, sums[:, :width], precision=HIGHEST, preferred_element_type=F32) * (1.0 / (NY * NC))
    p_basis = jnp.dot(inverse, p_total[...], precision=HIGHEST, preferred_element_type=F32)
    compressed = lax.dot_general(p_basis, q_next, TN, precision=HIGHEST, preferred_element_type=F32)
    q_out[...] = q_next
    compressed_out[...] = compressed
    error_out[...] = merged[...] - compressed


def finish(place, mine, other, p_total, merged):
    rank = p_total.shape[0]
    return pl.pallas_call(
        finish_kernel,
        out_shape=(
            jax.ShapeDtypeStruct(merged.shape, F32),
            jax.ShapeDtypeStruct(merged.shape, F32),
            jax.ShapeDtypeStruct((rank, merged.shape[1]), F32),
        ),
        in_specs=[pl.BlockSpec(memory_space=pltpu.SMEM)] + [pl.BlockSpec(memory_space=pltpu.VMEM)] * 4,
        compiler_params=pltpu.CompilerParams(vmem_limit_bytes=32 * 1024 * 1024),
        name="finish",
    )(place, mine, other, p_total, merged)


def local(activations, cotangent, kv_weight, error_buffer, q_start):
    c, x, z = (lax.axis_index(a) for a in "cxz")
    place = jnp.stack([x, c, z] + [x ^ k for k in PARTNERS]).astype(jnp.int32)
    error = error_buffer[0]

    with jax.named_scope("exchange"):
        sub = kv_weight.shape[0] // NC
        line = lax.all_gather(kv_weight, "z", axis=0)
        packed = pack(place, activations, cotangent)
        pieces = [swap(packed[i], "x", NX, PARTNERS[i // 2]) for i in (0, 1, 4, 5, 2, 3)]

    with jax.named_scope("gradient"):
        part = gradient_terms(place, activations, cotangent, pieces)
        part, pieces, line = lax.optimization_barrier((part, pieces, line))
        gradient = lax.psum_scatter(part, "z", scatter_dimension=0, tiled=True)

    with jax.named_scope("weight"):
        halves = swaps(lax.dynamic_slice_in_dim(line, c * sub, sub, axis=1), "x", NX)

    with jax.named_scope("left"):
        left = left_terms(place, q_start, error, activations, cotangent, pieces)
        left = tree(list(lax.all_to_all(left, ("y", "c"), 0, 0, tiled=True)))
        left = tree(list(lax.all_to_all(left, "z", 0, 0, tiled=True)))
        left = jnp.broadcast_to(left[None], (NY * NC,) + left.shape)
        p_total = lax.all_to_all(left, ("y", "c"), 0, 0, tiled=True).reshape(q_start.shape[0], -1)
        p_total, halves = lax.optimization_barrier((p_total, halves))

    with jax.named_scope("weight"):
        weights = []
        for half in halves:
            weights += [half, swap(half, "c", NC, 1)]
        input_grad, flag = project(place, cotangent, weights[:NX], 0, ())
        input_grad, last_flag = project(place, cotangent, weights[NX:], NX // 2, (input_grad,))
        swapped = tree([half[0, :16, :128] for half in weights[1::2]])

    with jax.named_scope("sums"):
        merged, keep, give = right_terms(place, swapped, gradient, error, p_total)
        keep = keep + swap(give, "c", NC, 1)
        keep = tree(swaps(keep, "y", NY))
        keep = add_after(flag, swaps(keep, "x", NX))
        keep = keep + swap(keep, "z", NZ, 1)
        keep = add_after(last_flag, [keep] + [swap(keep, "z", NZ, k) for k in (2, 4, 6)])
        other = swap(keep, "c", NC, 1)

    with jax.named_scope("finish"):
        error_next, compressed, q_next = finish(place, keep, other, p_total, merged)
    return (input_grad, error_next[None], compressed, q_next)


def solution(mesh):
    fine = Mesh(mesh.devices.reshape(NY, NC, NX, NZ), ("y", "c", "x", "z"))
    dp, fsdp = ("y", "c"), ("x", "z")
    return jax.shard_map(
        local,
        mesh=fine,
        in_specs=(P(dp + fsdp, None), P(dp + fsdp, None), P(fsdp, None), P(dp, fsdp, None), P()),
        out_specs=(P(dp + fsdp, None), P(dp, fsdp, None), P(fsdp, None), P()),
        check_vma=False,
    )
```
